32 devices in a mesh: groups: 2 (over y), dp: 4 (over z), sub: 2 (over x), pair: 2 (over core).
Axes of the slice: x: 2, y: 2, z: 4, core: 2. Of those that a mesh axis runs over, the one named last changes fastest.
Arguments:
- query_inputs: bfloat16 [2048, 4096], P(('groups', 'dp', 'sub', 'pair')), parts along dimension 0, may hold values from -0.31835938 to 0.31835938
- query_gradient: bfloat16 [2048, 4096], P(('groups', 'dp', 'sub', 'pair')), parts along dimension 0, may hold values from -0.31835938 to 0.31835938
- query_sequence_index: int32 [2048], P(('groups', 'dp', 'sub', 'pair')), parts along dimension 0, may hold values from 0 to 15, never falling along the last dimension, each value on 1 to 128 neighbouring positions
- training_inputs: bfloat16 [32, 128, 4096], P(('groups', 'dp', 'pair')), parts along dimension 0, may hold values from -0.31835938 to 0.31835938
- training_gradient: bfloat16 [32, 128, 4096], P(('groups', 'dp', 'pair')), parts along dimension 0, may hold values from -0.31835938 to 0.31835938
- training_length: int32 [32], P(('groups', 'dp', 'pair')), parts along dimension 0, may hold values from 1 to 128, 1536 in all
- adapter_down_map: bfloat16 [4096, 16], replicated, may hold values from -0.796875 to 0.796875
- adapter_up_map: bfloat16 [4096, 16], replicated, may hold values from -0.796875 to 0.796875
Outputs:
- scores: float32 [32, 16], P(('groups', 'sub'), ('dp', 'pair')), parts along dimension 0
The draws below stay inside these ranges and needn't reach their ends.
There are 2 independent parts, one for each index of `groups`. The reference program is written for one: setup_inputs(seed, part) draws one part's arguments, and reference() takes and returns one part's arrays. A program takes and returns all parts, laid end to end along the dimension named above; an argument that names none is the same for every part. Nothing has to cross between parts.
Inputs may be any that keep to these rules, and one draw needn't show every extreme that they name: `query_sequence_index`: ids do not fall along the tokens; every id from 0 to 15 is held by 1 to 128 tokens, one id by exactly 128. `training_length`: they sum to 1536; at least one sequence fills all 128 slots.
All inputs are finite; a program needn't handle non-finite values. No bound on the sum of `training_length` on one device may be relied on, other than what follows from the above.
Results may differ from the reference program's by a relative error of at most 0.004.
Values may be sent and summed in bfloat16 or wider, within the bound.
No kernel may reach another device: no remote copies, remote signals or barrier semaphores. Data moves between devices by JAX's collectives and lax.ppermute only.
A program may use at most 64 MiB of HBM per device.

```python
import math
import jax
import jax.numpy as jnp
import numpy as np
from jax import lax

MODEL_WIDTH = 4096
ADAPTER_RANK = 16
TSLOT = 128
QMOST = 128
NTSEQ = 16
QTOK = 1024
NQSEQ = 16


def shard_levels(stream_key, dims, pieces, smallest, largest):
    def one(dim, parts):
        steps = jax.random.uniform(jax.random.fold_in(jax.random.fold_in(stream_key, 6), dim), (parts,), jnp.float32, smallest / len(pieces), largest / len(pieces))
        return jnp.repeat(jnp.exp(steps), dims[dim] // parts).reshape((-1,) + (1,) * (len(dims) - dim - 1))

    gain = one(*pieces[0])
    for cut in pieces[1:]:
        gain = gain * one(*cut)
    return gain


def length_profile(number_of, total, reach, lean):
    weights = [(1 << 20) // math.isqrt(standing ** lean) + 1 for standing in range(2, number_of + 1)]
    rest, holding = total - reach - (number_of - 1), [1] * (number_of - 1)
    while rest > 0:
        movable = [i for i in range(number_of - 1) if holding[i] < reach]
        whole, left = sum([weights[i] for i in movable]), rest
        for i in movable:
            addition = min(reach - holding[i], max(1, left * weights[i] // whole), rest)
            holding[i] = holding[i] + addition
            rest = rest - addition
    return np.array([reach] + holding)


def uneven(key, count, total, most, lean):
    if count == 2:
        one = jax.random.randint(key, (), max(1, total - most), min(most, total - 1) + 1)
        return jnp.stack([one, total - one])
    sizes = jnp.asarray(length_profile(count, total, most, lean), jnp.int32)
    twos = (count - 1) // 2
    giver, taker = sizes[1:1 + 2 * twos:2], sizes[2:2 + 2 * twos:2]
    margin = jnp.minimum(giver - 1, most - taker)
    shifted = jax.random.randint(jax.random.fold_in(key, 1), (twos,), 0, 1 << 20) % (margin + 1)
    sizes = sizes.at[1:1 + 2 * twos:2].set(giver - shifted).at[2:2 + 2 * twos:2].set(taker + shifted)
    return sizes[jax.random.permutation(jax.random.fold_in(key, 2), count)]


def gaussian(stream_key, extent, width, most, shards=(), kind=jnp.bfloat16):
    entries = width * jax.random.normal(stream_key, extent, jnp.float32)
    if shards:
        entries = entries * shard_levels(stream_key, extent, shards, -0.22, 0.18)
    return jnp.clip(entries, -most, most).astype(kind)


def setup_inputs(seed: int = 0, part: int = 0) -> dict:
    arg_keys = jax.random.split(jax.random.key(seed), 9)
    part_keys = jax.random.split(jax.random.fold_in(arg_keys[8], part), 9)
    return {
        "query_inputs": gaussian(part_keys[0], (QTOK, MODEL_WIDTH), 0.04, 0.31835938, ((0, 16),)),
        "query_gradient": gaussian(part_keys[1], (QTOK, MODEL_WIDTH), 0.04, 0.31835938, ((0, 16),)),
        "query_sequence_index": jnp.searchsorted(jnp.cumsum(uneven(part_keys[2], NQSEQ, QTOK, QMOST, 2)), jnp.arange(QTOK), side="right").astype(jnp.int32),
        "training_inputs": gaussian(part_keys[3], (NTSEQ, TSLOT, MODEL_WIDTH), 0.04, 0.31835938, ((0, 8),)),
        "training_gradient": gaussian(part_keys[4], (NTSEQ, TSLOT, MODEL_WIDTH), 0.04, 0.31835938, ((0, 8),)),
        "training_length": uneven(part_keys[5], NTSEQ, NTSEQ * TSLOT * 3 // 4, TSLOT, 1).astype(jnp.int32),
        "adapter_down_map": gaussian(arg_keys[6], (MODEL_WIDTH, ADAPTER_RANK), 0.1, 0.796875),
        "adapter_up_map": gaussian(arg_keys[7], (MODEL_WIDTH, ADAPTER_RANK), 0.1, 0.796875),
    }


def reduced_rank(values, weights):
    return jnp.dot(values, weights, preferred_element_type=jnp.float32).astype(jnp.bfloat16)


def reference(query_inputs, query_gradient, query_sequence_index, training_inputs, training_gradient, training_length, adapter_down_map, adapter_up_map):
    query_down_map = reduced_rank(query_inputs, adapter_down_map)
    query_up_map = reduced_rank(query_gradient, adapter_up_map)

    def one_sequence(inputs):
        position_inputs, position_gradient, length = inputs
        position_down_map = reduced_rank(position_inputs, adapter_down_map)
        position_up_map = reduced_rank(position_gradient, adapter_up_map)
        gram_acts = jnp.dot(query_inputs, position_inputs.T, preferred_element_type=jnp.float32)
        gram_grads = jnp.dot(query_gradient, position_gradient.T, preferred_element_type=jnp.float32)
        gram_down = jnp.dot(query_down_map, position_down_map.T, preferred_element_type=jnp.float32)
        gram_up = jnp.dot(query_up_map, position_up_map.T, preferred_element_type=jnp.float32)
        pair_term = gram_grads * gram_down + gram_up * gram_acts
        live_mask = (jnp.arange(TSLOT, dtype=jnp.int32) < length).astype(jnp.float32)
        return jnp.sum(pair_term * live_mask[None, :], axis=1)

    per_token = lax.map(one_sequence, (training_inputs, training_gradient, training_length))
    return jax.ops.segment_sum(per_token.T, query_sequence_index, num_segments=NQSEQ)
```

```python
import functools

import jax
import jax.numpy as jnp
from jax import lax
from jax.experimental import pallas as pl
from jax.experimental.pallas import tpu as pltpu
from jax.sharding import PartitionSpec as P

QMEAN = 64
EXTRA = 16
VMEM = pl.BlockSpec(memory_space=pltpu.VMEM)
SMEM = pl.BlockSpec(memory_space=pltpu.SMEM)
HBM = pl.BlockSpec(memory_space=pl.ANY)
LIMIT = 48 * 1024 * 1024


def rows_by_rows(left, right, **kwargs):
    return lax.dot_general(
        left, right, (((1,), (1,)), ((), ())), preferred_element_type=jnp.float32, **kwargs
    )


def swap(value, axis, distance):
    count = lax.axis_size(axis)
    return lax.ppermute(value, axis, [(source, source ^ distance) for source in range(count)])


def share_start(nlo, nsub, dlo, dsub, width):
    low = (lax.axis_index("dp") % nlo) ^ dlo
    part = low * nsub + (lax.axis_index("sub") ^ dsub)
    return pl.multiple_of(part * width, width)


def query_kernel(nlo, nsub, inputs, gradient, ids, down, up, *shares):
    tokens, features = inputs.shape
    width = features // (nlo * nsub)
    low_down = rows_by_rows(down[...], inputs[...]).astype(jnp.bfloat16)
    low_up = rows_by_rows(up[...], gradient[...]).astype(jnp.bfloat16)
    rank = low_down.shape[0]
    id_rows = jnp.broadcast_to(ids[...].astype(jnp.bfloat16), (EXTRA, tokens))
    for place, share in enumerate(shares):
        columns = pl.ds(share_start(nlo, nsub, place // nsub, place % nsub, width), width)
        share[0:tokens, :] = inputs[:, columns]
        share[tokens : 2 * tokens, :] = gradient[:, columns]
        share[2 * tokens :, :] = jnp.zeros((EXTRA, width), jnp.bfloat16)
        share[2 * tokens : 2 * tokens + rank, 0:tokens] = low_down
        share[2 * tokens : 2 * tokens + rank, 64 : 64 + tokens] = low_up
        share[2 * tokens :, 128 : 128 + tokens] = id_rows


def training_kernel(nlo, nsub, lengths, inputs, gradient, down, up, *rest):
    outs, (held_inputs, held_gradient, sems) = rest[:nlo], rest[nlo:]
    sequences, slots, features = inputs.shape
    rows = sequences * slots
    rank = down.shape[0]
    width = features // (nlo * nsub)
    pieces = 4
    step = features // pieces
    copies = []
    for array, (source, target) in enumerate(((inputs, held_inputs), (gradient, held_gradient))):
        for piece in range(pieces):
            columns = pl.ds(piece * step, step)
            copy = pltpu.make_async_copy(
                source.at[:, :, columns], target.at[:, :, columns], sems.at[array, piece]
            )
            copy.start()
            copies.append(copy)

    live = jnp.concatenate(
        [
            jnp.concatenate(
                [
                    (lax.broadcasted_iota(jnp.int32, (rank, slots), 1) < lengths[row])
                    if row == column
                    else jnp.zeros((rank, slots), jnp.bool_)
                    for column in range(sequences)
                ],
                axis=1,
            ).astype(jnp.float32)
            for row in range(sequences)
        ],
        axis=0,
    )
    low = []
    for array, (target, weights) in enumerate(((held_inputs, down), (held_gradient, up))):
        total = jnp.zeros((rank, rows), jnp.float32)
        for piece in range(pieces):
            copies[array * pieces + piece].wait()
            columns = pl.ds(piece * step, step)
            total += rows_by_rows(weights[:, columns], target[:, :, columns].reshape(rows, step))
        rounded = total.astype(jnp.bfloat16).astype(jnp.float32)
        low.append((jnp.concatenate([rounded] * sequences, axis=0) * live).astype(jnp.bfloat16))

    for place, out in enumerate(outs):
        columns = pl.ds(share_start(nlo, nsub, place, 0, width), width)
        for half, (factor, target) in enumerate(((low[0], held_gradient), (low[1], held_inputs))):
            product = jnp.dot(
                factor,
                target[:, :, columns].reshape(rows, width),
                preferred_element_type=jnp.float32,
            )
            out[half * sequences * rank : (half + 1) * sequences * rank, :] = product.astype(
                jnp.bfloat16
            )


def score_kernel(nblocks, ndp, nsub, rank, count, *refs):
    blocks, grads = refs[:nblocks], refs[nblocks : nblocks + ndp]
    out, tokens_in, tokens_gr, extras, grad_down, grad_up, sems = refs[nblocks + ndp :]
    tokens = (blocks[0].shape[0] - EXTRA) // 2
    per = grads[0].shape[0] // 2
    copies = []
    for place, block in enumerate(blocks):
        for part, (start, size, target) in enumerate(
            ((0, tokens, tokens_in), (tokens, tokens, tokens_gr))
        ):
            copies.append(
                pltpu.make_async_copy(
                    block.at[pl.ds(start, size), :],
                    target.at[pl.ds(place * size, size), :],
                    sems.at[3 * place + part],
                )
            )
        copies.append(
            pltpu.make_async_copy(
                block.at[pl.ds(2 * tokens, EXTRA), pl.ds(0, 256)],
                extras.at[place],
                sems.at[3 * place + 2],
            )
        )
    for place, grad in enumerate(grads):
        for part, target in enumerate((grad_down, grad_up)):
            copies.append(
                pltpu.make_async_copy(
                    grad.at[pl.ds(part * per, per), :],
                    target.at[pl.ds(place * per, per), :],
                    sems.at[3 * nblocks + 2 * place + part],
                )
            )
    for copy in copies:
        copy.start()
    for copy in copies:
        copy.wait()

    gathered = [extras[place] for place in range(nblocks)]

    def along(lane):
        return jnp.concatenate(
            [piece[:, lane : lane + tokens].astype(jnp.float32) for piece in gathered], axis=1
        )

    low_down, low_up, ids = along(0)[:rank], along(64)[:rank], along(128)[0:1]
    sequences = ndp * per // rank
    total = nblocks * tokens
    product = rows_by_rows(grad_down[...], tokens_gr[...]).reshape(
        sequences, rank, total
    ) * low_down[None]
    product += rows_by_rows(grad_up[...], tokens_in[...]).reshape(
        sequences, rank, total
    ) * low_up[None]
    per_token = jnp.sum(product, axis=1)
    owned = count // nsub
    place = lax.broadcasted_iota(jnp.int32, (count, total), 0)
    number = ((place // owned) ^ lax.axis_index("sub")) * owned + place % owned
    one_hot = (ids.astype(jnp.int32) == number).astype(jnp.float32)
    out[...] = rows_by_rows(one_hot, per_token, precision=lax.Precision.HIGHEST)


def per_device(
    query_inputs,
    query_gradient,
    query_sequence_index,
    training_inputs,
    training_gradient,
    training_length,
    adapter_down_map,
    adapter_up_map,
):
    tokens, features = query_inputs.shape
    sequences, slots, _ = training_inputs.shape
    rank = adapter_down_map.shape[1]
    ndp, nsub, npair = (lax.axis_size(name) for name in ("dp", "sub", "pair"))
    nlo = 2
    width = features // (nlo * nsub)
    count = tokens * ndp * nsub * npair // QMEAN
    down, up = adapter_down_map.T, adapter_up_map.T
    params = pltpu.CompilerParams(vmem_limit_bytes=LIMIT)

    shares = pl.pallas_call(
        functools.partial(query_kernel, nlo, nsub),
        out_shape=[jax.ShapeDtypeStruct((2 * tokens + EXTRA, width), jnp.bfloat16)] * (nlo * nsub),
        in_specs=[VMEM] * 5,
        out_specs=[VMEM] * (nlo * nsub),
        compiler_params=params,
        name="query_shares",
    )(query_inputs, query_gradient, query_sequence_index.reshape(1, tokens), down, up)
    blocks = [shares[0]]
    for place in range(1, nlo * nsub):
        dlo, dsub = place // nsub, place % nsub
        pairs = [
            (i * nsub + j, (i ^ dlo) * nsub + (j ^ dsub)) for i in range(ndp) for j in range(nsub)
        ]
        blocks.append(lax.ppermute(shares[place], ("dp", "sub"), pairs))

    grads = pl.pallas_call(
        functools.partial(training_kernel, nlo, nsub),
        out_shape=[jax.ShapeDtypeStruct((2 * sequences * rank, width), jnp.bfloat16)] * nlo,
        in_specs=[SMEM, HBM, HBM, VMEM, VMEM],
        out_specs=[VMEM] * nlo,
        scratch_shapes=[
            pltpu.VMEM((sequences, slots, features), jnp.bfloat16),
            pltpu.VMEM((sequences, slots, features), jnp.bfloat16),
            pltpu.SemaphoreType.DMA((2, 4)),
        ],
        compiler_params=params,
        name="training_gradients",
    )(training_length, training_inputs, training_gradient, down, up)
    every = [grads[0]] + [swap(grads[distance % nlo], "dp", distance) for distance in range(1, ndp)]

    blocks += [swap(block, "pair", 1) for block in blocks]
    nblocks = len(blocks)
    scores = pl.pallas_call(
        functools.partial(score_kernel, nblocks, ndp, nsub, rank, count),
        out_shape=jax.ShapeDtypeStruct((count, ndp * sequences), jnp.float32),
        in_specs=[HBM] * (nblocks + ndp),
        out_specs=VMEM,
        scratch_shapes=[
            pltpu.VMEM((nblocks * tokens, width), jnp.bfloat16),
            pltpu.VMEM((nblocks * tokens, width), jnp.bfloat16),
            pltpu.VMEM((nblocks, EXTRA, 256), jnp.bfloat16),
            pltpu.VMEM((ndp * sequences * rank, width), jnp.bfloat16),
            pltpu.VMEM((ndp * sequences * rank, width), jnp.bfloat16),
            pltpu.SemaphoreType.DMA((3 * nblocks + 2 * ndp,)),
        ],
        compiler_params=params,
        name="scores",
    )(*blocks, *every)

    scores = scores.reshape(nsub, count // nsub, ndp, sequences)
    distance = nsub // 2
    while distance:
        scores = scores[:distance] + swap(scores[distance:], "sub", distance)
        distance //= 2
    scores = scores[0]
    distance = ndp // 2
    while distance:
        scores = scores[:, :distance] + swap(scores[:, distance:], "dp", distance)
        distance //= 2
    return scores[:, 0]


def solution(mesh):
    placed = (
        P(("groups", "dp", "sub", "pair"), None),
        P(("groups", "dp", "sub", "pair"), None),
        P(("groups", "dp", "sub", "pair")),
        P(("groups", "dp", "pair"), None, None),
        P(("groups", "dp", "pair"), None, None),
        P(("groups", "dp", "pair")),
        P(),
        P(),
    )
    return jax.shard_map(
        per_device,
        mesh=mesh,
        in_specs=placed,
        out_specs=P(("groups", "sub"), ("dp", "pair")),
        check_vma=False,
    )
```

```python
import functools

import jax
import jax.numpy as jnp
from jax import lax
from jax.experimental import pallas as pl
from jax.experimental.pallas import tpu as pltpu
from jax.sharding import PartitionSpec as P

QMEAN = 64
EXTRA = 16
FAR_COST = 40000
VMEM = pl.BlockSpec(memory_space=pltpu.VMEM)
SMEM = pl.BlockSpec(memory_space=pltpu.SMEM)
HBM = pl.BlockSpec(memory_space=pltpu.HBM)
LIMIT = 48 * 1024 * 1024


def rows_by_rows(left, right, **kwargs):
    return lax.dot_general(
        left, right, (((1,), (1,)), ((), ())), preferred_element_type=jnp.float32, **kwargs
    )


def in_hbm(*arrays):
    return [pltpu.with_memory_space_constraint(array, pltpu.HBM) for array in arrays]


def swap(value, axis, distance):
    count = lax.axis_size(axis)
    return lax.ppermute(value, axis, [(source, source ^ distance) for source in range(count)])


def share_start(nlo, nsub, dlo, dsub, width):
    low = (lax.axis_index("dp") % nlo) ^ dlo
    part = low * nsub + (lax.axis_index("sub") ^ dsub)
    return pl.multiple_of(part * width, width)


def query_kernel(nlo, nsub, inputs, gradient, ids, down, up, *rest):
    shares, (held_inputs, held_gradient, held_ids, held_down, held_up, sems) = rest[:-6], rest[-6:]
    tokens, features = inputs.shape
    width = features // (nlo * nsub)
    copies = [
        pltpu.make_async_copy(source, target, sems.at[place])
        for place, (source, target) in enumerate(
            (
                (inputs, held_inputs),
                (down, held_down),
                (gradient, held_gradient),
                (up, held_up),
                (ids, held_ids),
            )
        )
    ]
    for copy in copies:
        copy.start()
    copies[0].wait()
    copies[1].wait()
    low_down = rows_by_rows(held_down[...], held_inputs[...]).astype(jnp.bfloat16)
    for copy in copies[2:]:
        copy.wait()
    low_up = rows_by_rows(held_up[...], held_gradient[...]).astype(jnp.bfloat16)
    rank = low_down.shape[0]
    id_rows = jnp.broadcast_to(held_ids[...].astype(jnp.bfloat16), (EXTRA, tokens))
    for place, share in enumerate(shares):
        columns = pl.ds(share_start(nlo, nsub, place // nsub, place % nsub, width), width)
        share[0:tokens, :] = held_inputs[:, columns]
        share[tokens : 2 * tokens, :] = held_gradient[:, columns]
        share[2 * tokens :, :] = jnp.zeros((EXTRA, width), jnp.bfloat16)
        share[2 * tokens : 2 * tokens + rank, 0:tokens] = low_down
        share[2 * tokens : 2 * tokens + rank, 64 : 64 + tokens] = low_up
        share[2 * tokens :, 128 : 128 + tokens] = id_rows


def training_kernel(nlo, nsub, length_source, inputs, gradient, down, up, *rest):
    outs, scratch = rest[:nlo], rest[nlo:]
    held_inputs, held_gradient, held_down, held_up, lengths, sems, map_sems = scratch
    sequences, slots, features = inputs.shape
    rows = sequences * slots
    rank = down.shape[0]
    width = features // (nlo * nsub)
    pieces = sems.shape[1]
    step = features // pieces
    maps = [
        pltpu.make_async_copy(down, held_down, map_sems.at[0]),
        pltpu.make_async_copy(up, held_up, map_sems.at[1]),
        pltpu.make_async_copy(length_source, lengths, map_sems.at[2]),
    ]
    maps[2].start()
    copies = []
    for array, (source, target) in enumerate(((inputs, held_inputs), (gradient, held_gradient))):
        maps[array].start()
        for piece in range(pieces):
            columns = pl.ds(piece * step, step)
            copy = pltpu.make_async_copy(
                source.at[:, :, columns], target.at[:, :, columns], sems.at[array, piece]
            )
            copy.start()
            copies.append(copy)

    maps[2].wait()
    live = jnp.concatenate(
        [
            jnp.concatenate(
                [
                    (lax.broadcasted_iota(jnp.int32, (rank, slots), 1) < lengths[row])
                    if row == column
                    else jnp.zeros((rank, slots), jnp.bool_)
                    for column in range(sequences)
                ],
                axis=1,
            ).astype(jnp.float32)
            for row in range(sequences)
        ],
        axis=0,
    )
    low = []
    for array, (target, weights) in enumerate(((held_inputs, held_down), (held_gradient, held_up))):
        total = jnp.zeros((rank, rows), jnp.float32)
        maps[array].wait()
        for piece in range(pieces):
            copies[array * pieces + piece].wait()
            columns = pl.ds(piece * step, step)
            total += rows_by_rows(weights[:, columns], target[:, :, columns].reshape(rows, step))
        rounded = total.astype(jnp.bfloat16).astype(jnp.float32)
        low.append((jnp.concatenate([rounded] * sequences, axis=0) * live).astype(jnp.bfloat16))

    for place, out in enumerate(outs):
        columns = pl.ds(share_start(nlo, nsub, place, 0, width), width)
        for half, (factor, target) in enumerate(((low[0], held_gradient), (low[1], held_inputs))):
            product = jnp.dot(
                factor,
                target[:, :, columns].reshape(rows, width),
                preferred_element_type=jnp.float32,
            )
            out[half * sequences * rank : (half + 1) * sequences * rank, :] = product.astype(
                jnp.bfloat16
            )


def stack_kernel(*refs):
    blocks, (grad, out, near) = refs[:-3], refs[-3:]
    nblocks = len(blocks)
    tokens = (blocks[0].shape[0] - EXTRA) // 2
    near[...] = grad[...]
    for place, block in enumerate(blocks):
        out[place * tokens : (place + 1) * tokens, :] = block[0:tokens, :]
        start = (nblocks + place) * tokens
        out[start : start + tokens, :] = block[tokens : 2 * tokens, :]
        start = 2 * nblocks * tokens + place * EXTRA
        out[start : start + EXTRA, :] = block[2 * tokens :, :]


def score_kernel(nblocks, nsub, rank, owned, stacks, grads, *refs):
    token_refs, grad_refs, base, out = (
        refs[:stacks],
        refs[stacks : stacks + grads],
        refs[stacks + grads : -1],
        refs[-1],
    )
    total = (token_refs[0].shape[0] - nblocks * EXTRA) // 2
    tokens = total // nblocks
    per = grad_refs[0].shape[0] // 2
    sequences = grads * per // rank
    grad_down = jnp.concatenate([grad[:per] for grad in grad_refs], axis=0)
    grad_up = jnp.concatenate([grad[per:] for grad in grad_refs], axis=0)
    number = lax.broadcasted_iota(jnp.int32, (owned, total), 0)
    scores = [ref[...] for ref in base] or [jnp.zeros(out.shape, jnp.float32)]
    scores = [scores[0][place] for place in range(nsub)]
    for stack in token_refs:
        pieces = [
            stack[2 * total + place * EXTRA : 2 * total + (place + 1) * EXTRA, 0:256].astype(
                jnp.float32
            )
            for place in range(nblocks)
        ]

        def along(lane, pieces=pieces):
            return jnp.concatenate([piece[:, lane : lane + tokens] for piece in pieces], axis=1)

        low_down, low_up = along(0)[:rank], along(64)[:rank]
        ids = along(128)[0:1].astype(jnp.int32)
        product = rows_by_rows(grad_down, stack[total : 2 * total, :]).reshape(
            sequences, rank, total
        ) * low_down[None]
        product += rows_by_rows(grad_up, stack[0:total, :]).reshape(
            sequences, rank, total
        ) * low_up[None]
        per_token = jnp.sum(product, axis=1)
        for place in range(nsub):
            first = (place ^ lax.axis_index("sub")) * owned
            one_hot = (ids == number + first).astype(jnp.float32)
            scores[place] += rows_by_rows(per_token, one_hot, precision=lax.Precision.HIGHEST)
    for place in range(nsub):
        out[place] = scores[place]


def per_device(
    query_inputs,
    query_gradient,
    query_sequence_index,
    training_inputs,
    training_gradient,
    training_length,
    adapter_down_map,
    adapter_up_map,
):
    tokens, features = query_inputs.shape
    sequences, slots, _ = training_inputs.shape
    rank = adapter_down_map.shape[1]
    ndp, nsub, npair = (lax.axis_size(name) for name in ("dp", "sub", "pair"))
    nlo = 2
    width = features // (nlo * nsub)
    count = tokens * ndp * nsub * npair // QMEAN
    down, up = adapter_down_map.T, adapter_up_map.T
    params = pltpu.CompilerParams(vmem_limit_bytes=LIMIT)

    shares = pl.pallas_call(
        functools.partial(query_kernel, nlo, nsub),
        out_shape=[jax.ShapeDtypeStruct((2 * tokens + EXTRA, width), jnp.bfloat16)] * (nlo * nsub),
        in_specs=[HBM] * 5,
        out_specs=[VMEM] * (nlo * nsub),
        scratch_shapes=[
            pltpu.VMEM((tokens, features), jnp.bfloat16),
            pltpu.VMEM((tokens, features), jnp.bfloat16),
            pltpu.VMEM((1, tokens), jnp.int32),
            pltpu.VMEM((rank, features), jnp.bfloat16),
            pltpu.VMEM((rank, features), jnp.bfloat16),
            pltpu.SemaphoreType.DMA((5,)),
        ],
        compiler_params=params,
        name="query_shares",
    )(*in_hbm(query_inputs, query_gradient, query_sequence_index.reshape(1, tokens), down, up))
    blocks = [shares[0]]
    for place in sorted(range(1, nlo * nsub), key=lambda place: place < nsub):
        dlo, dsub = place // nsub, place % nsub
        pairs = [
            (i * nsub + j, (i ^ dlo) * nsub + (j ^ dsub)) for i in range(ndp) for j in range(nsub)
        ]
        blocks.append(lax.ppermute(shares[place], ("dp", "sub"), pairs))

    grads = pl.pallas_call(
        functools.partial(training_kernel, nlo, nsub),
        out_shape=[jax.ShapeDtypeStruct((2 * sequences * rank, width), jnp.bfloat16)] * nlo,
        in_specs=[HBM] * 5,
        out_specs=[VMEM] * nlo,
        scratch_shapes=[
            pltpu.VMEM((sequences, slots, features), jnp.bfloat16),
            pltpu.VMEM((sequences, slots, features), jnp.bfloat16),
            pltpu.VMEM((rank, features), jnp.bfloat16),
            pltpu.VMEM((rank, features), jnp.bfloat16),
            pltpu.SMEM((sequences,), jnp.int32),
            pltpu.SemaphoreType.DMA((2, 4)),
            pltpu.SemaphoreType.DMA((3,)),
        ],
        cost_estimate=pl.CostEstimate(
            flops=12 * sequences * slots * features * rank,
            bytes_accessed=12 * sequences * slots * features,
            transcendentals=0,
        ),
        compiler_params=params,
        name="training_gradients",
    )(*in_hbm(training_length, training_inputs, training_gradient, down, up))
    nblocks = len(blocks)
    rows = nblocks * (2 * tokens + EXTRA)
    stack, near = pl.pallas_call(
        stack_kernel,
        out_shape=[
            jax.ShapeDtypeStruct((rows, width), jnp.bfloat16),
            jax.ShapeDtypeStruct(grads[-1].shape, jnp.bfloat16),
        ],
        in_specs=[VMEM] * (nblocks + 1),
        out_specs=[VMEM] * 2,
        compiler_params=params,
        name="token_stack",
    )(*blocks, grads[-1])
    far = [swap(grads[distance % nlo], "dp", distance) for distance in range(2, ndp)]
    owned = count // nsub

    def partial(stacks, some, base, flops, name):
        return pl.pallas_call(
            functools.partial(score_kernel, nblocks, nsub, rank, owned, len(stacks), len(some)),
            out_shape=jax.ShapeDtypeStruct((nsub, len(some) * sequences, owned), jnp.float32),
            in_specs=[VMEM] * (len(stacks) + len(some) + len(base)),
            out_specs=VMEM,
            compiler_params=params,
            cost_estimate=pl.CostEstimate(
                flops=flops, bytes_accessed=3 * stack.size, transcendentals=0
            ),
            name=name,
        )(*stacks, *some, *base)

    far_scores = partial([stack], far, [], FAR_COST * stack.size, "far_scores_part")
    other = swap(stack, "pair", 1)
    far_scores = partial([other], far, [far_scores], stack.size, "far_scores")
    near_scores = partial(
        [stack, other], [grads[0], swap(near, "dp", 1)], [], stack.size, "near_scores"
    )
    distance = ndp // 2
    while distance > 1:
        kept = (distance - 2) * sequences
        received = swap(far_scores[:, kept:], "dp", distance)
        near_scores += received[:, : 2 * sequences]
        far_scores = far_scores[:, :kept] + received[:, 2 * sequences :]
        distance //= 2
    distance = nsub // 2
    while distance:
        near_scores = near_scores[:distance] + swap(near_scores[distance:], "sub", distance)
        distance //= 2
    scores = near_scores[0]
    return (scores[:sequences] + swap(scores[sequences:], "dp", 1)).T


def solution(mesh):
    placed = (
        P(("groups", "dp", "sub", "pair"), None),
        P(("groups", "dp", "sub", "pair"), None),
        P(("groups", "dp", "sub", "pair")),
        P(("groups", "dp", "pair"), None, None),
        P(("groups", "dp", "pair"), None, None),
        P(("groups", "dp", "pair")),
        P(),
        P(),
    )
    return jax.shard_map(
        per_device,
        mesh=mesh,
        in_specs=placed,
        out_specs=P(("groups", "sub"), ("dp", "pair")),
        check_vma=False,
    )
```

```python
import functools

import jax
import jax.numpy as jnp
from jax import lax
from jax.experimental import pallas as pl
from jax.experimental.pallas import tpu as pltpu
from jax.sharding import PartitionSpec as P

QMEAN = 64
EXTRA = 128
KEPT = 48
FAR_COST = 40000
VMEM = pl.BlockSpec(memory_space=pltpu.VMEM)
SMEM = pl.BlockSpec(memory_space=pltpu.SMEM)
HBM = pl.BlockSpec(memory_space=pltpu.HBM)
LIMIT = 48 * 1024 * 1024


def rows_by_rows(left, right, **kwargs):
    return lax.dot_general(
        left, right, (((1,), (1,)), ((), ())), preferred_element_type=jnp.float32, **kwargs
    )


def in_hbm(*arrays):
    return [pltpu.with_memory_space_constraint(array, pltpu.HBM) for array in arrays]


def swap(value, axis, distance):
    count = lax.axis_size(axis)
    return lax.ppermute(value, axis, [(source, source ^ distance) for source in range(count)])


def share_start(nlo, nsub, dlo, dsub, width):
    low = (lax.axis_index("dp") % nlo) ^ dlo
    part = low * nsub + (lax.axis_index("sub") ^ dsub)
    return pl.multiple_of(part * width, width)


def query_kernel(nlo, nsub, inputs, gradient, ids, down, up, *rest):
    shares, (held_inputs, held_gradient, held_ids, held_down, held_up, sems) = rest[:-6], rest[-6:]
    tokens, features = inputs.shape
    width = features // (nlo * nsub)
    copies = [
        pltpu.make_async_copy(source, target, sems.at[place])
        for place, (source, target) in enumerate(
            (
                (inputs, held_inputs),
                (down, held_down),
                (gradient, held_gradient),
                (up, held_up),
                (ids, held_ids),
            )
        )
    ]
    for copy in copies:
        copy.start()
    starts = [
        share_start(nlo, nsub, place // nsub, place % nsub, width) for place in range(len(shares))
    ]
    copies[0].wait()
    for start, share in zip(starts, shares):
        share[:, 0:width] = held_inputs[:, pl.ds(start, width)]
    copies[1].wait()
    low_down = rows_by_rows(held_down[...], held_inputs[...])
    copies[2].wait()
    for start, share in zip(starts, shares):
        share[:, width : 2 * width] = held_gradient[:, pl.ds(start, width)]
    copies[3].wait()
    copies[4].wait()
    low_up = rows_by_rows(held_up[...], held_gradient[...])
    rank = low_down.shape[0]
    id_rows = jnp.broadcast_to(held_ids[...].astype(jnp.float32), (EXTRA - 2 * rank, tokens))
    extras = jnp.concatenate([low_down, low_up, id_rows], axis=0).T.astype(jnp.bfloat16)
    for share in shares:
        share[:, 2 * width :] = extras


def training_kernel(nlo, nsub, length_source, inputs, gradient, down, up, *rest):
    outs, scratch = rest[:nlo], rest[nlo:]
    held_inputs, held_gradient, held_down, held_up, lengths, sems, map_sems = scratch
    sequences, slots, features = inputs.shape
    rows = sequences * slots
    rank = down.shape[0]
    width = features // (nlo * nsub)
    pieces = sems.shape[1]
    step = features // pieces
    maps = [
        pltpu.make_async_copy(down, held_down, map_sems.at[0]),
        pltpu.make_async_copy(up, held_up, map_sems.at[1]),
        pltpu.make_async_copy(length_source, lengths, map_sems.at[2]),
    ]
    maps[2].start()
    maps[0].start()
    maps[1].start()
    held = (held_inputs, held_gradient)
    copies = []
    for piece in range(pieces):
        columns = pl.ds(piece * step, step)
        for array, source in enumerate((inputs, gradient)):
            copy = pltpu.make_async_copy(
                source.at[:, :, columns], held[array].at[:, :, columns], sems.at[array, piece]
            )
            copy.start()
            copies.append(copy)

    maps[2].wait()
    live = jnp.concatenate(
        [
            jnp.concatenate(
                [
                    (lax.broadcasted_iota(jnp.int32, (rank, slots), 1) < lengths[row])
                    if row == column
                    else jnp.zeros((rank, slots), jnp.bool_)
                    for column in range(sequences)
                ],
                axis=1,
            ).astype(jnp.float32)
            for row in range(sequences)
        ],
        axis=0,
    )
    maps[0].wait()
    maps[1].wait()
    totals = [[0.0] * sequences, [0.0] * sequences]
    for piece in range(pieces):
        columns = pl.ds(piece * step, step)
        for copy in copies[2 * piece : 2 * piece + 2]:
            copy.wait()
        for array, weights in enumerate((held_down, held_up)):
            for row in range(sequences):
                totals[array][row] += rows_by_rows(weights[:, columns], held[array][row, :, columns])
    low = []
    for parts in totals:
        rounded = jnp.concatenate(parts, axis=1).astype(jnp.bfloat16).astype(jnp.float32)
        low.append((jnp.concatenate([rounded] * sequences, axis=0) * live).astype(jnp.bfloat16))

    for place, out in enumerate(outs):
        columns = pl.ds(share_start(nlo, nsub, place, 0, width), width)
        for half, (factor, target) in enumerate(((low[0], held_gradient), (low[1], held_inputs))):
            product = jnp.dot(
                factor,
                target[:, :, columns].reshape(rows, width),
                preferred_element_type=jnp.float32,
            )
            out[half * sequences * rank : (half + 1) * sequences * rank, :] = product.astype(
                jnp.bfloat16
            )


def stack_kernel(*refs):
    blocks, out = refs[:-1], refs[-1]
    tokens = blocks[0].shape[0]
    width = out.shape[1]
    total = len(blocks) * tokens
    extras = []
    for place, block in enumerate(blocks):
        out[place * tokens : (place + 1) * tokens, :] = block[:, 0:width]
        start = total + place * tokens
        out[start : start + tokens, :] = block[:, width : 2 * width]
        extras.append(block[:, 2 * width :].astype(jnp.float32).T[:KEPT].astype(jnp.bfloat16))
    chunk = min(width, total)
    for place in range(total // chunk):
        some = extras[place * chunk // tokens : (place + 1) * chunk // tokens]
        start = 2 * total + place * KEPT
        out[start : start + KEPT, 0:chunk] = jnp.concatenate(some, axis=1)


def gather_kernel(*refs):
    blocks, out = refs[:-1], refs[-1]
    for place, block in enumerate(blocks):
        half = block.shape[0] // 2
        out[place * half : (place + 1) * half, :] = block[:half, :]
        start = (len(blocks) + place) * half
        out[start : start + half, :] = block[half:, :]


def copy_kernel(source, _, target):
    target[...] = source[...]


def score_kernel(total, nsub, rank, owned, stacks, *refs):
    token_refs, grads, out = refs[:stacks], refs[stacks], refs[-1]
    chunk = min(total, token_refs[0].shape[1])
    per = grads.shape[0] // 2
    sequences = per // rank
    grad_down, grad_up = grads[:per], grads[per:]
    number = lax.broadcasted_iota(jnp.int32, (owned, total), 0)
    scores = [jnp.zeros((sequences, owned), jnp.float32)] * nsub
    for stack in token_refs:
        extras = jnp.concatenate(
            [
                stack[2 * total + place * KEPT : 2 * total + (place + 1) * KEPT, 0:chunk]
                for place in range(total // chunk)
            ],
            axis=1,
        ).astype(jnp.float32)
        low_down, low_up = extras[:rank], extras[rank : 2 * rank]
        ids = extras[2 * rank : 2 * rank + 1].astype(jnp.int32)
        product = rows_by_rows(grad_down, stack[total : 2 * total, :]).reshape(
            sequences, rank, total
        ) * low_down[None]
        product += rows_by_rows(grad_up, stack[0:total, :]).reshape(
            sequences, rank, total
        ) * low_up[None]
        per_token = jnp.sum(product, axis=1)
        for place in range(nsub):
            first = (place ^ lax.axis_index("sub")) * owned
            one_hot = (ids == number + first).astype(jnp.float32)
            scores[place] += rows_by_rows(per_token, one_hot, precision=lax.Precision.HIGHEST)
    for place in range(nsub):
        out[place] = scores[place]


def per_device(
    query_inputs,
    query_gradient,
    query_sequence_index,
    training_inputs,
    training_gradient,
    training_length,
    adapter_down_map,
    adapter_up_map,
):
    tokens, features = query_inputs.shape
    sequences, slots, _ = training_inputs.shape
    rank = adapter_down_map.shape[1]
    ndp, nsub, npair = (lax.axis_size(name) for name in ("dp", "sub", "pair"))
    nlo = 2
    width = features // (nlo * nsub)
    count = tokens * ndp * nsub * npair // QMEAN
    down, up = adapter_down_map.T, adapter_up_map.T
    params = pltpu.CompilerParams(vmem_limit_bytes=LIMIT)

    shares = pl.pallas_call(
        functools.partial(query_kernel, nlo, nsub),
        out_shape=[jax.ShapeDtypeStruct((tokens, 2 * width + EXTRA), jnp.bfloat16)] * (nlo * nsub),
        in_specs=[HBM] * 5,
        out_specs=[VMEM] * (nlo * nsub),
        scratch_shapes=[
            pltpu.VMEM((tokens, features), jnp.bfloat16),
            pltpu.VMEM((tokens, features), jnp.bfloat16),
            pltpu.VMEM((1, tokens), jnp.int32),
            pltpu.VMEM((rank, features), jnp.bfloat16),
            pltpu.VMEM((rank, features), jnp.bfloat16),
            pltpu.SemaphoreType.DMA((5,)),
        ],
        compiler_params=params,
        name="query_shares",
    )(*in_hbm(query_inputs, query_gradient, query_sequence_index.reshape(1, tokens), down, up))
    blocks = [shares[0]]
    for place in sorted(range(1, nlo * nsub), key=lambda place: place < nsub):
        dlo, dsub = place // nsub, place % nsub
        pairs = [
            (i * nsub + j, (i ^ dlo) * nsub + (j ^ dsub)) for i in range(ndp) for j in range(nsub)
        ]
        blocks.append(lax.ppermute(shares[place], ("dp", "sub"), pairs))

    grads = pl.pallas_call(
        functools.partial(training_kernel, nlo, nsub),
        out_shape=[jax.ShapeDtypeStruct((2 * sequences * rank, width), jnp.bfloat16)] * nlo,
        in_specs=[HBM] * 5,
        out_specs=[VMEM] * nlo,
        scratch_shapes=[
            pltpu.VMEM((sequences, slots, features), jnp.bfloat16),
            pltpu.VMEM((sequences, slots, features), jnp.bfloat16),
            pltpu.VMEM((rank, features), jnp.bfloat16),
            pltpu.VMEM((rank, features), jnp.bfloat16),
            pltpu.SMEM((sequences,), jnp.int32),
            pltpu.SemaphoreType.DMA((2, 2)),
            pltpu.SemaphoreType.DMA((3,)),
        ],
        cost_estimate=pl.CostEstimate(
            flops=12 * sequences * slots * features * rank,
            bytes_accessed=12 * sequences * slots * features,
            transcendentals=0,
        ),
        compiler_params=params,
        name="training_gradients",
    )(*in_hbm(training_length, training_inputs, training_gradient, down, up))
    nblocks = len(blocks)
    total = nblocks * tokens
    rows = 2 * total + KEPT * max(1, total // width)
    def call(kernel, shape, *operands, name, flops=0):
        return pl.pallas_call(
            kernel,
            out_shape=jax.ShapeDtypeStruct(*shape),
            in_specs=[VMEM] * len(operands),
            out_specs=VMEM,
            compiler_params=params,
            cost_estimate=pl.CostEstimate(
                flops=flops, bytes_accessed=rows * width, transcendentals=0
            ),
            name=name,
        )(*operands)

    stack = call(stack_kernel, ((rows, width), jnp.bfloat16), *blocks, name="token_stack")
    far = [swap(grads[distance % nlo], "dp", distance) for distance in range(2, ndp)]
    owned = count // nsub
    per = grads[0].shape[0]

    far = call(
        gather_kernel,
        ((per * (ndp - 2), width), jnp.bfloat16),
        *far,
        name="far_gradients",
        flops=FAR_COST * stack.size,
    )
    other = swap(stack, "pair", 1)
    near = call(copy_kernel, ((per, width), jnp.bfloat16), grads[-1], stack, name="near_gradient")
    near = call(
        gather_kernel,
        ((2 * per, width), jnp.bfloat16),
        grads[0],
        swap(near, "dp", 1),
        name="near_gradients",
    )

    def partial(some, name):
        return call(
            functools.partial(score_kernel, total, nsub, rank, owned, 2),
            ((nsub, some.shape[0] // (2 * rank), owned), jnp.float32),
            stack,
            other,
            some,
            name=name,
        )

    far_scores = partial(far, "far_scores")
    near_scores = partial(near, "near_scores")
    distance = ndp // 2
    while distance > 1:
        kept = (distance - 2) * sequences
        received = swap(far_scores[:, kept:], "dp", distance)
        near_scores += received[:, : 2 * sequences]
        far_scores = far_scores[:, :kept] + received[:, 2 * sequences :]
        distance //= 2
    distance = nsub // 2
    while distance:
        near_scores = near_scores[:distance] + swap(near_scores[distance:], "sub", distance)
        distance //= 2
    scores = near_scores[0]
    return (scores[:sequences] + swap(scores[sequences:], "dp", 1)).T


def solution(mesh):
    placed = (
        P(("groups", "dp", "sub", "pair"), None),
        P(("groups", "dp", "sub", "pair"), None),
        P(("groups", "dp", "sub", "pair")),
        P(("groups", "dp", "pair"), None, None),
        P(("groups", "dp", "pair"), None, None),
        P(("groups", "dp", "pair")),
        P(),
        P(),
    )
    return jax.shard_map(
        per_device,
        mesh=mesh,
        in_specs=placed,
        out_specs=P(("groups", "sub"), ("dp", "pair")),
        check_vma=False,
    )
```

```python
import functools

import jax
import jax.numpy as jnp
from jax import lax
from jax.experimental import pallas as pl
from jax.experimental.pallas import tpu as pltpu
from jax.sharding import PartitionSpec as P

QMEAN = 64
EXTRA = 128
KEPT = 48
FAR_COST = 40000
VMEM = pl.BlockSpec(memory_space=pltpu.VMEM)
SMEM = pl.BlockSpec(memory_space=pltpu.SMEM)
HBM = pl.BlockSpec(memory_space=pltpu.HBM)
LIMIT = 48 * 1024 * 1024


def rows_by_rows(left, right, **kwargs):
    return lax.dot_general(
        left, right, (((1,), (1,)), ((), ())), preferred_element_type=jnp.float32, **kwargs
    )


def in_hbm(*arrays):
    return [pltpu.with_memory_space_constraint(array, pltpu.HBM) for array in arrays]


def swap(value, axis, distance):
    count = lax.axis_size(axis)
    return lax.ppermute(value, axis, [(source, source ^ distance) for source in range(count)])


def share_start(nlo, nsub, dlo, dsub, width):
    low = (lax.axis_index("dp") % nlo) ^ dlo
    part = low * nsub + (lax.axis_index("sub") ^ dsub)
    return pl.multiple_of(part * width, width)


def query_kernel(nlo, nsub, inputs, gradient, ids, down, up, *rest):
    shares, (held_inputs, held_gradient, held_ids, held_down, held_up, sems) = rest[:-6], rest[-6:]
    tokens, features = inputs.shape
    width = features // (nlo * nsub)
    copies = [
        pltpu.make_async_copy(source, target, sems.at[place])
        for place, (source, target) in enumerate(
            (
                (inputs, held_inputs),
                (down, held_down),
                (gradient, held_gradient),
                (up, held_up),
                (ids, held_ids),
            )
        )
    ]
    for copy in copies:
        copy.start()
    starts = [
        share_start(nlo, nsub, place // nsub, place % nsub, width) for place in range(len(shares))
    ]
    copies[0].wait()
    for start, share in zip(starts, shares):
        share[:, 0:width] = held_inputs[:, pl.ds(start, width)]
    for copy in copies[1:]:
        copy.wait()
    low_down, low_up = 0.0, 0.0
    for half in range(2):
        columns = pl.ds(half * features // 2, features // 2)
        low_down += rows_by_rows(held_down[:, columns], held_inputs[:, columns])
        low_up += rows_by_rows(held_up[:, columns], held_gradient[:, columns])
    for start, share in zip(starts, shares):
        share[:, width : 2 * width] = held_gradient[:, pl.ds(start, width)]
    rank = low_down.shape[0]
    id_rows = jnp.broadcast_to(held_ids[...].astype(jnp.float32), (EXTRA - 2 * rank, tokens))
    extras = jnp.concatenate([low_down, low_up, id_rows], axis=0).T.astype(jnp.bfloat16)
    for share in shares:
        share[:, 2 * width :] = extras


def training_kernel(nlo, nsub, length_source, inputs, gradient, down, up, *rest):
    outs, scratch = rest[:nlo], rest[nlo:]
    held_inputs, held_gradient, held_down, held_up, lengths, sems, map_sems = scratch
    sequences, slots, features = inputs.shape
    rows = sequences * slots
    rank = down.shape[0]
    width = features // (nlo * nsub)
    pieces = sems.shape[1]
    step = features // pieces
    maps = [
        pltpu.make_async_copy(down, held_down, map_sems.at[0]),
        pltpu.make_async_copy(up, held_up, map_sems.at[1]),
        pltpu.make_async_copy(length_source, lengths, map_sems.at[2]),
    ]
    maps[2].start()
    maps[0].start()
    maps[1].start()
    held = (held_inputs, held_gradient)
    copies = []
    for piece in range(pieces):
        columns = pl.ds(piece * step, step)
        for array, source in enumerate((inputs, gradient)):
            copy = pltpu.make_async_copy(
                source.at[:, :, columns], held[array].at[:, :, columns], sems.at[array, piece]
            )
            copy.start()
            copies.append(copy)

    maps[2].wait()
    live = jnp.concatenate(
        [
            jnp.concatenate(
                [
                    (lax.broadcasted_iota(jnp.int32, (rank, slots), 1) < lengths[row])
                    if row == column
                    else jnp.zeros((rank, slots), jnp.bool_)
                    for column in range(sequences)
                ],
                axis=1,
            ).astype(jnp.float32)
            for row in range(sequences)
        ],
        axis=0,
    )
    maps[0].wait()
    maps[1].wait()
    totals = [[0.0] * sequences, [0.0] * sequences]
    for piece in range(pieces):
        columns = pl.ds(piece * step, step)
        for copy in copies[2 * piece : 2 * piece + 2]:
            copy.wait()
        for array, weights in enumerate((held_down, held_up)):
            for row in range(sequences):
                totals[array][row] += rows_by_rows(weights[:, columns], held[array][row, :, columns])
    low = []
    for parts in totals:
        rounded = jnp.concatenate(parts, axis=1).astype(jnp.bfloat16).astype(jnp.float32)
        low.append((jnp.concatenate([rounded] * sequences, axis=0) * live).astype(jnp.bfloat16))

    for place, out in enumerate(outs):
        columns = pl.ds(share_start(nlo, nsub, place, 0, width), width)
        for half, (factor, target) in enumerate(((low[0], held_gradient), (low[1], held_inputs))):
            product = jnp.dot(
                factor,
                target[:, :, columns].reshape(rows, width),
                preferred_element_type=jnp.float32,
            )
            out[half * sequences * rank : (half + 1) * sequences * rank, :] = product.astype(
                jnp.bfloat16
            )


def stack_kernel(*refs):
    blocks, out = refs[:-1], refs[-1]
    tokens = blocks[0].shape[0]
    width = out.shape[1]
    total = len(blocks) * tokens
    extras = []
    for place, block in enumerate(blocks):
        out[place * tokens : (place + 1) * tokens, :] = block[:, 0:width]
        start = total + place * tokens
        out[start : start + tokens, :] = block[:, width : 2 * width]
        extras.append(block[:, 2 * width :].astype(jnp.float32).T[:KEPT].astype(jnp.bfloat16))
    chunk = min(width, total)
    for place in range(total // chunk):
        some = extras[place * chunk // tokens : (place + 1) * chunk // tokens]
        start = 2 * total + place * KEPT
        out[start : start + KEPT, 0:chunk] = jnp.concatenate(some, axis=1)


def gather_kernel(*refs):
    blocks, out = refs[:-1], refs[-1]
    for place, block in enumerate(blocks):
        half = block.shape[0] // 2
        out[place * half : (place + 1) * half, :] = block[:half, :]
        start = (len(blocks) + place) * half
        out[start : start + half, :] = block[half:, :]


def copy_kernel(source, _, target):
    target[...] = source[...]


def score_kernel(total, nsub, rank, owned, stacks, *refs):
    token_refs, grads, out = refs[:stacks], refs[stacks], refs[-1]
    chunk = min(total, token_refs[0].shape[1])
    per = grads.shape[0] // 2
    sequences = per // rank
    grad_down, grad_up = grads[:per], grads[per:]
    number = lax.broadcasted_iota(jnp.int32, (owned, total), 0)
    scores = [jnp.zeros((sequences, owned), jnp.float32)] * nsub
    for stack in token_refs:
        extras = jnp.concatenate(
            [
                stack[2 * total + place * KEPT : 2 * total + (place + 1) * KEPT, 0:chunk]
                for place in range(total // chunk)
            ],
            axis=1,
        ).astype(jnp.float32)
        low_down, low_up = extras[:rank], extras[rank : 2 * rank]
        ids = extras[2 * rank : 2 * rank + 1].astype(jnp.int32)
        product = rows_by_rows(grad_down, stack[total : 2 * total, :]).reshape(
            sequences, rank, total
        ) * low_down[None]
        product += rows_by_rows(grad_up, stack[0:total, :]).reshape(
            sequences, rank, total
        ) * low_up[None]
        per_token = jnp.sum(product, axis=1)
        for place in range(nsub):
            first = (place ^ lax.axis_index("sub")) * owned
            one_hot = (ids == number + first).astype(jnp.float32)
            scores[place] += rows_by_rows(per_token, one_hot, precision=lax.Precision.HIGHEST)
    for place in range(nsub):
        out[place] = scores[place]


def per_device(
    query_inputs,
    query_gradient,
    query_sequence_index,
    training_inputs,
    training_gradient,
    training_length,
    adapter_down_map,
    adapter_up_map,
):
    tokens, features = query_inputs.shape
    sequences, slots, _ = training_inputs.shape
    rank = adapter_down_map.shape[1]
    ndp, nsub, npair = (lax.axis_size(name) for name in ("dp", "sub", "pair"))
    nlo = 2
    width = features // (nlo * nsub)
    count = tokens * ndp * nsub * npair // QMEAN
    down, up = adapter_down_map.T, adapter_up_map.T
    params = pltpu.CompilerParams(vmem_limit_bytes=LIMIT)

    shares = pl.pallas_call(
        functools.partial(query_kernel, nlo, nsub),
        out_shape=[jax.ShapeDtypeStruct((tokens, 2 * width + EXTRA), jnp.bfloat16)] * (nlo * nsub),
        in_specs=[HBM] * 5,
        out_specs=[VMEM] * (nlo * nsub),
        scratch_shapes=[
            pltpu.VMEM((tokens, features), jnp.bfloat16),
            pltpu.VMEM((tokens, features), jnp.bfloat16),
            pltpu.VMEM((1, tokens), jnp.int32),
            pltpu.VMEM((rank, features), jnp.bfloat16),
            pltpu.VMEM((rank, features), jnp.bfloat16),
            pltpu.SemaphoreType.DMA((5,)),
        ],
        compiler_params=params,
        name="query_shares",
    )(*in_hbm(query_inputs, query_gradient, query_sequence_index.reshape(1, tokens), down, up))
    blocks = [shares[0]]
    for place in sorted(range(1, nlo * nsub), key=lambda place: place < nsub):
        dlo, dsub = place // nsub, place % nsub
        pairs = [
            (i * nsub + j, (i ^ dlo) * nsub + (j ^ dsub)) for i in range(ndp) for j in range(nsub)
        ]
        blocks.append(lax.ppermute(shares[place], ("dp", "sub"), pairs))

    grads = pl.pallas_call(
        functools.partial(training_kernel, nlo, nsub),
        out_shape=[jax.ShapeDtypeStruct((2 * sequences * rank, width), jnp.bfloat16)] * nlo,
        in_specs=[HBM] * 5,
        out_specs=[VMEM] * nlo,
        scratch_shapes=[
            pltpu.VMEM((sequences, slots, features), jnp.bfloat16),
            pltpu.VMEM((sequences, slots, features), jnp.bfloat16),
            pltpu.VMEM((rank, features), jnp.bfloat16),
            pltpu.VMEM((rank, features), jnp.bfloat16),
            pltpu.SMEM((sequences,), jnp.int32),
            pltpu.SemaphoreType.DMA((2, 2)),
            pltpu.SemaphoreType.DMA((3,)),
        ],
        cost_estimate=pl.CostEstimate(
            flops=12 * sequences * slots * features * rank,
            bytes_accessed=12 * sequences * slots * features,
            transcendentals=0,
        ),
        compiler_params=params,
        name="training_gradients",
    )(*in_hbm(training_length, training_inputs, training_gradient, down, up))
    nblocks = nlo * nsub
    total = nblocks * tokens
    rows = 2 * total + KEPT * max(1, total // width)
    def call(kernel, shape, *operands, name, flops=0):
        return pl.pallas_call(
            kernel,
            out_shape=jax.ShapeDtypeStruct(*shape),
            in_specs=[VMEM] * len(operands),
            out_specs=VMEM,
            compiler_params=params,
            cost_estimate=pl.CostEstimate(
                flops=flops, bytes_accessed=rows * width, transcendentals=0
            ),
            name=name,
        )(*operands)

    stack = call(stack_kernel, ((rows, width), jnp.bfloat16), *blocks, name="token_stack")
    far = [swap(grads[distance % nlo], "dp", distance) for distance in range(2, ndp)]
    owned = count // nsub
    per = grads[0].shape[0]

    far = call(
        gather_kernel,
        ((per * (ndp - 2), width), jnp.bfloat16),
        *far,
        name="far_gradients",
        flops=FAR_COST * stack.size,
    )
    other = swap(stack, "pair", 1)
    near = call(copy_kernel, ((per, width), jnp.bfloat16), grads[-1], stack, name="near_gradient")
    near = call(
        gather_kernel,
        ((2 * per, width), jnp.bfloat16),
        grads[0],
        swap(near, "dp", 1),
        name="near_gradients",
    )

    def partial(some, name):
        return call(
            functools.partial(score_kernel, total, nsub, rank, owned, 2),
            ((nsub, some.shape[0] // (2 * rank), owned), jnp.float32),
            stack,
            other,
            some,
            name=name,
        )

    far_scores = partial(far, "far_scores")
    near_scores = partial(near, "near_scores")
    distance = ndp // 2
    while distance > 1:
        kept = (distance - 2) * sequences
        received = swap(far_scores[:, kept:], "dp", distance)
        near_scores += received[:, : 2 * sequences]
        far_scores = far_scores[:, :kept] + received[:, 2 * sequences :]
        distance //= 2
    distance = nsub // 2
    while distance:
        near_scores = near_scores[:distance] + swap(near_scores[distance:], "sub", distance)
        distance //= 2
    scores = near_scores[0]
    return (scores[:sequences] + swap(scores[sequences:], "dp", 1)).T


def solution(mesh):
    placed = (
        P(("groups", "dp", "sub", "pair"), None),
        P(("groups", "dp", "sub", "pair"), None),
        P(("groups", "dp", "sub", "pair")),
        P(("groups", "dp", "pair"), None, None),
        P(("groups", "dp", "pair"), None, None),
        P(("groups", "dp", "pair")),
        P(),
        P(),
    )
    return jax.shard_map(
        per_device,
        mesh=mesh,
        in_specs=placed,
        out_specs=P(("groups", "sub"), ("dp", "pair")),
        check_vma=False,
    )
```

```python
import functools

import jax
import jax.numpy as jnp
from jax import lax
from jax.experimental import pallas as pl
from jax.experimental.pallas import tpu as pltpu
from jax.sharding import PartitionSpec as P

QMEAN = 64
EXTRA = 128
KEPT = 48
FAR_COST = 40000
VMEM = pl.BlockSpec(memory_space=pltpu.VMEM)
SMEM = pl.BlockSpec(memory_space=pltpu.SMEM)
HBM = pl.BlockSpec(memory_space=pltpu.HBM)
LIMIT = 48 * 1024 * 1024


def rows_by_rows(left, right, **kwargs):
    return lax.dot_general(
        left, right, (((1,), (1,)), ((), ())), preferred_element_type=jnp.float32, **kwargs
    )


def in_hbm(*arrays):
    return [pltpu.with_memory_space_constraint(array, pltpu.HBM) for array in arrays]


def swap(value, axis, distance):
    count = lax.axis_size(axis)
    return lax.ppermute(value, axis, [(source, source ^ distance) for source in range(count)])


def share_start(nlo, nsub, dlo, dsub, width):
    low = (lax.axis_index("dp") % nlo) ^ dlo
    part = low * nsub + (lax.axis_index("sub") ^ dsub)
    return pl.multiple_of(part * width, width)


def query_kernel(nlo, nsub, inputs, gradient, ids, down, up, *rest):
    shares, (held_inputs, held_gradient, held_ids, held_down, held_up, sems) = rest[:-6], rest[-6:]
    tokens, features = inputs.shape
    width = features // (nlo * nsub)
    copies = [
        pltpu.make_async_copy(source, target, sems.at[place])
        for place, (source, target) in enumerate(
            (
                (inputs, held_inputs),
                (down, held_down),
                (gradient, held_gradient),
                (up, held_up),
                (ids, held_ids),
            )
        )
    ]
    for copy in copies:
        copy.start()
    starts = [
        share_start(nlo, nsub, place // nsub, place % nsub, width) for place in range(len(shares))
    ]
    copies[0].wait()
    for start, share in zip(starts, shares):
        share[:, 0:width] = held_inputs[:, pl.ds(start, width)]
    for copy in copies[1:]:
        copy.wait()
    low_down, low_up = 0.0, 0.0
    for half in range(2):
        columns = pl.ds(half * features // 2, features // 2)
        low_down += rows_by_rows(held_down[:, columns], held_inputs[:, columns])
        low_up += rows_by_rows(held_up[:, columns], held_gradient[:, columns])
    for start, share in zip(starts, shares):
        share[:, width : 2 * width] = held_gradient[:, pl.ds(start, width)]
    rank = low_down.shape[0]
    id_rows = jnp.broadcast_to(held_ids[...].astype(jnp.float32), (EXTRA - 2 * rank, tokens))
    extras = jnp.concatenate([low_down, low_up, id_rows], axis=0).T.astype(jnp.bfloat16)
    for share in shares:
        share[:, 2 * width :] = extras


def training_kernel(nlo, nsub, length_source, inputs, gradient, down, up, *rest):
    outs, scratch = rest[:nlo], rest[nlo:]
    held_inputs, held_gradient, held_down, held_up, lengths, sems, map_sems = scratch
    sequences, slots, features = inputs.shape
    rows = sequences * slots
    rank = down.shape[0]
    width = features // (nlo * nsub)
    pieces = sems.shape[1]
    step = features // pieces
    maps = [
        pltpu.make_async_copy(down, held_down, map_sems.at[0]),
        pltpu.make_async_copy(up, held_up, map_sems.at[1]),
        pltpu.make_async_copy(length_source, lengths, map_sems.at[2]),
    ]
    maps[2].start()
    maps[0].start()
    maps[1].start()
    held = (held_inputs, held_gradient)
    copies = []
    for piece in range(pieces):
        columns = pl.ds(piece * step, step)
        for array, source in enumerate((inputs, gradient)):
            copy = pltpu.make_async_copy(
                source.at[:, :, columns], held[array].at[:, :, columns], sems.at[array, piece]
            )
            copy.start()
            copies.append(copy)

    maps[2].wait()
    live = jnp.concatenate(
        [
            jnp.concatenate(
                [
                    (lax.broadcasted_iota(jnp.int32, (rank, slots), 1) < lengths[row])
                    if row == column
                    else jnp.zeros((rank, slots), jnp.bool_)
                    for column in range(sequences)
                ],
                axis=1,
            ).astype(jnp.float32)
            for row in range(sequences)
        ],
        axis=0,
    )
    maps[0].wait()
    maps[1].wait()
    totals = [[0.0] * sequences, [0.0] * sequences]
    for piece in range(pieces):
        columns = pl.ds(piece * step, step)
        for copy in copies[2 * piece : 2 * piece + 2]:
            copy.wait()
        for array, weights in enumerate((held_down, held_up)):
            for row in range(sequences):
                totals[array][row] += rows_by_rows(weights[:, columns], held[array][row, :, columns])
    low = []
    for parts in totals:
        rounded = jnp.concatenate(parts, axis=1).astype(jnp.bfloat16).astype(jnp.float32)
        low.append((jnp.concatenate([rounded] * sequences, axis=0) * live).astype(jnp.bfloat16))

    for place, out in enumerate(outs):
        columns = pl.ds(share_start(nlo, nsub, place, 0, width), width)
        for half, (factor, target) in enumerate(((low[0], held_gradient), (low[1], held_inputs))):
            product = jnp.dot(
                factor,
                target[:, :, columns].reshape(rows, width),
                preferred_element_type=jnp.float32,
            )
            out[half * sequences * rank : (half + 1) * sequences * rank, :] = product.astype(
                jnp.bfloat16
            )


def stack_kernel(*refs):
    blocks, out = refs[:-1], refs[-1]
    tokens = blocks[0].shape[0]
    width = out.shape[1]
    total = len(blocks) * tokens
    extras = []
    for place, block in enumerate(blocks):
        out[place * tokens : (place + 1) * tokens, :] = block[:, 0:width]
        start = total + place * tokens
        out[start : start + tokens, :] = block[:, width : 2 * width]
        extras.append(block[:, 2 * width :].astype(jnp.float32).T[:KEPT].astype(jnp.bfloat16))
    chunk = min(width, total)
    for place in range(total // chunk):
        some = extras[place * chunk // tokens : (place + 1) * chunk // tokens]
        start = 2 * total + place * KEPT
        out[start : start + KEPT, 0:chunk] = jnp.concatenate(some, axis=1)


def gather_kernel(*refs):
    blocks, out = refs[:-1], refs[-1]
    for place, block in enumerate(blocks):
        half = block.shape[0] // 2
        out[place * half : (place + 1) * half, :] = block[:half, :]
        start = (len(blocks) + place) * half
        out[start : start + half, :] = block[half:, :]


def move_kernel(source, target):
    target[...] = source[...]


def copy_kernel(source, _, target):
    target[...] = source[...]


def score_kernel(total, nsub, rank, owned, stacks, *refs):
    token_refs, grads, out = refs[:stacks], refs[stacks], refs[-1]
    chunk = min(total, token_refs[0].shape[1])
    per = grads.shape[0] // 2
    sequences = per // rank
    grad_down, grad_up = grads[:per], grads[per:]
    number = lax.broadcasted_iota(jnp.int32, (owned, total), 0)
    scores = [jnp.zeros((sequences, owned), jnp.float32)] * nsub
    for stack in token_refs:
        extras = jnp.concatenate(
            [
                stack[2 * total + place * KEPT : 2 * total + (place + 1) * KEPT, 0:chunk]
                for place in range(total // chunk)
            ],
            axis=1,
        ).astype(jnp.float32)
        low_down, low_up = extras[:rank], extras[rank : 2 * rank]
        ids = extras[2 * rank : 2 * rank + 1].astype(jnp.int32)
        product = rows_by_rows(grad_down, stack[total : 2 * total, :]).reshape(
            sequences, rank, total
        ) * low_down[None]
        product += rows_by_rows(grad_up, stack[0:total, :]).reshape(
            sequences, rank, total
        ) * low_up[None]
        per_token = jnp.sum(product, axis=1)
        for place in range(nsub):
            first = (place ^ lax.axis_index("sub")) * owned
            one_hot = (ids == number + first).astype(jnp.float32)
            scores[place] += rows_by_rows(per_token, one_hot, precision=lax.Precision.HIGHEST)
    for place in range(nsub):
        out[place] = scores[place]


def per_device(
    query_inputs,
    query_gradient,
    query_sequence_index,
    training_inputs,
    training_gradient,
    training_length,
    adapter_down_map,
    adapter_up_map,
):
    tokens, features = query_inputs.shape
    sequences, slots, _ = training_inputs.shape
    rank = adapter_down_map.shape[1]
    ndp, nsub, npair = (lax.axis_size(name) for name in ("dp", "sub", "pair"))
    nlo = 2
    width = features // (nlo * nsub)
    count = tokens * ndp * nsub * npair // QMEAN
    down, up = adapter_down_map.T, adapter_up_map.T
    params = pltpu.CompilerParams(vmem_limit_bytes=LIMIT)

    shares = pl.pallas_call(
        functools.partial(query_kernel, nlo, nsub),
        out_shape=[jax.ShapeDtypeStruct((tokens, 2 * width + EXTRA), jnp.bfloat16)] * (nlo * nsub),
        in_specs=[HBM] * 5,
        out_specs=[VMEM] * (nlo * nsub),
        scratch_shapes=[
            pltpu.VMEM((tokens, features), jnp.bfloat16),
            pltpu.VMEM((tokens, features), jnp.bfloat16),
            pltpu.VMEM((1, tokens), jnp.int32),
            pltpu.VMEM((rank, features), jnp.bfloat16),
            pltpu.VMEM((rank, features), jnp.bfloat16),
            pltpu.SemaphoreType.DMA((5,)),
        ],
        compiler_params=params,
        name="query_shares",
    )(*in_hbm(query_inputs, query_gradient, query_sequence_index.reshape(1, tokens), down, up))
    blocks = [shares[0]]
    for place in sorted(range(1, nlo * nsub), key=lambda place: place < nsub):
        dlo, dsub = place // nsub, place % nsub
        pairs = [
            (i * nsub + j, (i ^ dlo) * nsub + (j ^ dsub)) for i in range(ndp) for j in range(nsub)
        ]
        blocks.append(lax.ppermute(shares[place], ("dp", "sub"), pairs))

    grads = pl.pallas_call(
        functools.partial(training_kernel, nlo, nsub),
        out_shape=[jax.ShapeDtypeStruct((2 * sequences * rank, width), jnp.bfloat16)] * nlo,
        in_specs=[HBM] * 5,
        out_specs=[VMEM] * nlo,
        scratch_shapes=[
            pltpu.VMEM((sequences, slots, features), jnp.bfloat16),
            pltpu.VMEM((sequences, slots, features), jnp.bfloat16),
            pltpu.VMEM((rank, features), jnp.bfloat16),
            pltpu.VMEM((rank, features), jnp.bfloat16),
            pltpu.SMEM((sequences,), jnp.int32),
            pltpu.SemaphoreType.DMA((2, 2)),
            pltpu.SemaphoreType.DMA((3,)),
        ],
        cost_estimate=pl.CostEstimate(
            flops=12 * sequences * slots * features * rank,
            bytes_accessed=12 * sequences * slots * features,
            transcendentals=0,
        ),
        compiler_params=params,
        name="training_gradients",
    )(*in_hbm(training_length, training_inputs, training_gradient, down, up))
    nblocks = nlo * nsub
    total = nblocks * tokens
    rows = 2 * total + KEPT * max(1, total // width)
    def call(kernel, shape, *operands, name, flops=0):
        return pl.pallas_call(
            kernel,
            out_shape=jax.ShapeDtypeStruct(*shape),
            in_specs=[VMEM] * len(operands),
            out_specs=VMEM,
            compiler_params=params,
            cost_estimate=pl.CostEstimate(
                flops=flops, bytes_accessed=rows * width, transcendentals=0
            ),
            name=name,
        )(*operands)

    stack = call(stack_kernel, ((rows, width), jnp.bfloat16), *blocks, name="token_stack")
    far = [swap(grads[distance % nlo], "dp", distance) for distance in range(2, ndp)]
    owned = count // nsub
    per = grads[0].shape[0]

    far = call(
        gather_kernel,
        ((per * (ndp - 2), width), jnp.bfloat16),
        *far,
        name="far_gradients",
        flops=FAR_COST * stack.size,
    )
    other = swap(stack, "pair", 1)
    near = call(copy_kernel, ((per, width), jnp.bfloat16), grads[-1], stack, name="near_gradient")
    near = call(
        gather_kernel,
        ((2 * per, width), jnp.bfloat16),
        grads[0],
        swap(near, "dp", 1),
        name="near_gradients",
    )

    def partial(some, name):
        return call(
            functools.partial(score_kernel, total, nsub, rank, owned, 2),
            ((nsub, some.shape[0] // (2 * rank), owned), jnp.float32),
            stack,
            other,
            some,
            name=name,
        )

    far_scores = partial(far, "far_scores")
    near_scores = partial(near, "near_scores")
    def crossing(value, distance):
        pairs = [
            (i * npair + k, (i ^ distance) * npair + (k ^ 1))
            for i in range(ndp)
            for k in range(npair)
        ]
        return lax.ppermute(value, ("dp", "pair"), pairs)

    near_count = 2 * sequences
    distance = ndp // 2
    kept = (distance - 2) * sequences
    received = crossing(far_scores[:, kept:], distance)
    received = call(
        move_kernel,
        (received.shape, received.dtype),
        received,
        name="received_scores",
        flops=FAR_COST * stack.size,
    )
    near_scores = swap(near_scores, "pair", 1) + received[:, :near_count]
    if kept:
        far_scores = swap(far_scores[:, :kept], "pair", 1) + received[:, near_count:]
    distance //= 2
    while distance > 1:
        kept = (distance - 2) * sequences
        received = swap(far_scores[:, kept:], "dp", distance)
        near_scores += received[:, :near_count]
        far_scores = far_scores[:, :kept] + received[:, near_count:]
        distance //= 2
    distance = nsub // 2
    while distance:
        near_scores = near_scores[:distance] + swap(near_scores[distance:], "sub", distance)
        distance //= 2
    scores = near_scores[0]
    other = crossing(scores[sequences:], 1)
    return (swap(scores[:sequences], "pair", 1) + other).T


def solution(mesh):
    placed = (
        P(("groups", "dp", "sub", "pair"), None),
        P(("groups", "dp", "sub", "pair"), None),
        P(("groups", "dp", "sub", "pair")),
        P(("groups", "dp", "pair"), None, None),
        P(("groups", "dp", "pair"), None, None),
        P(("groups", "dp", "pair")),
        P(),
        P(),
    )
    return jax.shard_map(
        per_device,
        mesh=mesh,
        in_specs=placed,
        out_specs=P(("groups", "sub"), ("dp", "pair")),
        check_vma=False,
    )
```

```python
import functools

import jax
import jax.numpy as jnp
from jax import lax
from jax.experimental import pallas as pl
from jax.experimental.pallas import tpu as pltpu
from jax.sharding import PartitionSpec as P

QMEAN = 64
EXTRA = 128
KEPT = 48
FAR_COST = 40000
VMEM = pl.BlockSpec(memory_space=pltpu.VMEM)
SMEM = pl.BlockSpec(memory_space=pltpu.SMEM)
HBM = pl.BlockSpec(memory_space=pltpu.HBM)
LIMIT = 48 * 1024 * 1024


def rows_by_rows(left, right, **kwargs):
    return lax.dot_general(
        left, right, (((1,), (1,)), ((), ())), preferred_element_type=jnp.float32, **kwargs
    )


def in_hbm(*arrays):
    return [pltpu.with_memory_space_constraint(array, pltpu.HBM) for array in arrays]


def swap(value, axis, distance):
    count = lax.axis_size(axis)
    return lax.ppermute(value, axis, [(source, source ^ distance) for source in range(count)])


def share_start(nlo, nsub, dlo, dsub, width):
    low = (lax.axis_index("dp") % nlo) ^ dlo
    part = low * nsub + (lax.axis_index("sub") ^ dsub)
    return pl.multiple_of(part * width, width)


def query_kernel(nlo, nsub, inputs, gradient, ids, down, up, *rest):
    shares, (held_inputs, held_gradient, held_ids, held_down, held_up, sems) = rest[:-6], rest[-6:]
    tokens, features = inputs.shape
    width = features // (nlo * nsub)
    copies = [
        pltpu.make_async_copy(source, target, sems.at[place])
        for place, (source, target) in enumerate(
            (
                (inputs, held_inputs),
                (down, held_down),
                (gradient, held_gradient),
                (up, held_up),
                (ids, held_ids),
            )
        )
    ]
    for copy in copies:
        copy.start()
    starts = [
        share_start(nlo, nsub, place // nsub, place % nsub, width) for place in range(len(shares))
    ]
    copies[0].wait()
    for start, share in zip(starts, shares):
        share[:, 0:width] = held_inputs[:, pl.ds(start, width)]
    for copy in copies[1:]:
        copy.wait()
    low_down, low_up = 0.0, 0.0
    for half in range(2):
        columns = pl.ds(half * features // 2, features // 2)
        low_down += rows_by_rows(held_down[:, columns], held_inputs[:, columns])
        low_up += rows_by_rows(held_up[:, columns], held_gradient[:, columns])
    for start, share in zip(starts, shares):
        share[:, width : 2 * width] = held_gradient[:, pl.ds(start, width)]
    rank = low_down.shape[0]
    id_rows = jnp.broadcast_to(held_ids[...].astype(jnp.float32), (EXTRA - 2 * rank, tokens))
    extras = jnp.concatenate([low_down, low_up, id_rows], axis=0).T.astype(jnp.bfloat16)
    for share in shares:
        share[:, 2 * width :] = extras


def training_kernel(nlo, nsub, length_source, inputs, gradient, down, up, *rest):
    outs, scratch = rest[:nlo], rest[nlo:]
    held_inputs, held_gradient, held_down, held_up, lengths, sems, map_sems = scratch
    sequences, slots, features = inputs.shape
    rows = sequences * slots
    rank = down.shape[0]
    width = features // (nlo * nsub)
    pieces = sems.shape[1]
    step = features // pieces
    maps = [
        pltpu.make_async_copy(down, held_down, map_sems.at[0]),
        pltpu.make_async_copy(up, held_up, map_sems.at[1]),
        pltpu.make_async_copy(length_source, lengths, map_sems.at[2]),
    ]
    maps[2].start()
    maps[0].start()
    maps[1].start()
    held = (held_inputs, held_gradient)
    copies = []
    for piece in range(pieces):
        columns = pl.ds(piece * step, step)
        for array, source in enumerate((inputs, gradient)):
            copy = pltpu.make_async_copy(
                source.at[:, :, columns], held[array].at[:, :, columns], sems.at[array, piece]
            )
            copy.start()
            copies.append(copy)

    maps[2].wait()
    live = jnp.concatenate(
        [
            jnp.concatenate(
                [
                    (lax.broadcasted_iota(jnp.int32, (rank, slots), 1) < lengths[row])
                    if row == column
                    else jnp.zeros((rank, slots), jnp.bool_)
                    for column in range(sequences)
                ],
                axis=1,
            ).astype(jnp.float32)
            for row in range(sequences)
        ],
        axis=0,
    )
    maps[0].wait()
    maps[1].wait()
    totals = [[0.0] * sequences, [0.0] * sequences]
    for piece in range(pieces):
        columns = pl.ds(piece * step, step)
        for copy in copies[2 * piece : 2 * piece + 2]:
            copy.wait()
        for array, weights in enumerate((held_down, held_up)):
            for row in range(sequences):
                totals[array][row] += rows_by_rows(weights[:, columns], held[array][row, :, columns])
    low = []
    for parts in totals:
        rounded = jnp.concatenate(parts, axis=1).astype(jnp.bfloat16).astype(jnp.float32)
        low.append((jnp.concatenate([rounded] * sequences, axis=0) * live).astype(jnp.bfloat16))

    for place, out in enumerate(outs):
        columns = pl.ds(share_start(nlo, nsub, place, 0, width), width)
        for half, (factor, target) in enumerate(((low[0], held_gradient), (low[1], held_inputs))):
            product = jnp.dot(
                factor,
                target[:, :, columns].reshape(rows, width),
                preferred_element_type=jnp.float32,
            )
            out[half * sequences * rank : (half + 1) * sequences * rank, :] = product.astype(
                jnp.bfloat16
            )


def stack_kernel(*refs):
    blocks, out = refs[:-1], refs[-1]
    tokens = blocks[0].shape[0]
    width = out.shape[1]
    total = len(blocks) * tokens
    extras = []
    for place, block in enumerate(blocks):
        out[place * tokens : (place + 1) * tokens, :] = block[:, 0:width]
        start = total + place * tokens
        out[start : start + tokens, :] = block[:, width : 2 * width]
        extras.append(block[:, 2 * width :].astype(jnp.float32).T[:KEPT].astype(jnp.bfloat16))
    chunk = min(width, total)
    for place in range(total // chunk):
        some = extras[place * chunk // tokens : (place + 1) * chunk // tokens]
        start = 2 * total + place * KEPT
        out[start : start + KEPT, 0:chunk] = jnp.concatenate(some, axis=1)


def gather_kernel(*refs):
    blocks, out = refs[:-1], refs[-1]
    for place, block in enumerate(blocks):
        half = block.shape[0] // 2
        out[place * half : (place + 1) * half, :] = block[:half, :]
        start = (len(blocks) + place) * half
        out[start : start + half, :] = block[half:, :]


def copy_kernel(source, _, target):
    target[...] = source[...]


def score_kernel(total, nsub, rank, owned, stacks, *refs):
    token_refs, grads, out = refs[:stacks], refs[stacks], refs[-1]
    chunk = min(total, token_refs[0].shape[1])
    per = grads.shape[0] // 2
    sequences = per // rank
    grad_down, grad_up = grads[:per], grads[per:]
    number = lax.broadcasted_iota(jnp.int32, (owned, total), 0)
    scores = [jnp.zeros((sequences, owned), jnp.float32)] * nsub
    for stack in token_refs:
        extras = jnp.concatenate(
            [
                stack[2 * total + place * KEPT : 2 * total + (place + 1) * KEPT, 0:chunk]
                for place in range(total // chunk)
            ],
            axis=1,
        ).astype(jnp.float32)
        low_down, low_up = extras[:rank], extras[rank : 2 * rank]
        ids = extras[2 * rank : 2 * rank + 1].astype(jnp.int32)
        product = rows_by_rows(grad_down, stack[total : 2 * total, :]).reshape(
            sequences, rank, total
        ) * low_down[None]
        product += rows_by_rows(grad_up, stack[0:total, :]).reshape(
            sequences, rank, total
        ) * low_up[None]
        per_token = jnp.sum(product, axis=1)
        for place in range(nsub):
            first = (place ^ lax.axis_index("sub")) * owned
            one_hot = (ids == number + first).astype(jnp.float32)
            scores[place] += rows_by_rows(per_token, one_hot, precision=lax.Precision.HIGHEST)
    for place in range(nsub):
        out[place] = scores[place]


def per_device(
    query_inputs,
    query_gradient,
    query_sequence_index,
    training_inputs,
    training_gradient,
    training_length,
    adapter_down_map,
    adapter_up_map,
):
    tokens, features = query_inputs.shape
    sequences, slots, _ = training_inputs.shape
    rank = adapter_down_map.shape[1]
    ndp, nsub, npair = (lax.axis_size(name) for name in ("dp", "sub", "pair"))
    nlo = 2
    width = features // (nlo * nsub)
    count = tokens * ndp * nsub * npair // QMEAN
    down, up = adapter_down_map.T, adapter_up_map.T
    params = pltpu.CompilerParams(vmem_limit_bytes=LIMIT)

    def crossing(value, axis, distance):
        pairs = [
            (i * npair + k, (i ^ distance) * npair + (k ^ 1))
            for i in range(lax.axis_size(axis))
            for k in range(npair)
        ]
        return lax.ppermute(value, (axis, "pair"), pairs)

    shares = pl.pallas_call(
        functools.partial(query_kernel, nlo, nsub),
        out_shape=[jax.ShapeDtypeStruct((tokens, 2 * width + EXTRA), jnp.bfloat16)] * (nlo * nsub),
        in_specs=[HBM] * 5,
        out_specs=[VMEM] * (nlo * nsub),
        scratch_shapes=[
            pltpu.VMEM((tokens, features), jnp.bfloat16),
            pltpu.VMEM((tokens, features), jnp.bfloat16),
            pltpu.VMEM((1, tokens), jnp.int32),
            pltpu.VMEM((rank, features), jnp.bfloat16),
            pltpu.VMEM((rank, features), jnp.bfloat16),
            pltpu.SemaphoreType.DMA((5,)),
        ],
        compiler_params=params,
        name="query_shares",
    )(*in_hbm(query_inputs, query_gradient, query_sequence_index.reshape(1, tokens), down, up))
    blocks = [shares[0]]
    for place in sorted(range(1, nlo * nsub), key=lambda place: place < nsub):
        dlo, dsub = place // nsub, place % nsub
        flip = dlo & (dsub > 0)
        pairs = []
        for i in range(ndp):
            for j in range(nsub):
                for k in range(npair):
                    target = ((i ^ dlo) * nsub + (j ^ dsub)) * npair + (k ^ flip)
                    pairs.append(((i * nsub + j) * npair + k, target))
        blocks.append(lax.ppermute(shares[place], ("dp", "sub", "pair"), pairs))

    grads = pl.pallas_call(
        functools.partial(training_kernel, nlo, nsub),
        out_shape=[jax.ShapeDtypeStruct((2 * sequences * rank, width), jnp.bfloat16)] * nlo,
        in_specs=[HBM] * 5,
        out_specs=[VMEM] * nlo,
        scratch_shapes=[
            pltpu.VMEM((sequences, slots, features), jnp.bfloat16),
            pltpu.VMEM((sequences, slots, features), jnp.bfloat16),
            pltpu.VMEM((rank, features), jnp.bfloat16),
            pltpu.VMEM((rank, features), jnp.bfloat16),
            pltpu.SMEM((sequences,), jnp.int32),
            pltpu.SemaphoreType.DMA((2, 2)),
            pltpu.SemaphoreType.DMA((3,)),
        ],
        cost_estimate=pl.CostEstimate(
            flops=12 * sequences * slots * features * rank,
            bytes_accessed=12 * sequences * slots * features,
            transcendentals=0,
        ),
        compiler_params=params,
        name="training_gradients",
    )(*in_hbm(training_length, training_inputs, training_gradient, down, up))
    nblocks = nlo * nsub
    total = nblocks * tokens
    rows = 2 * total + KEPT * max(1, total // width)
    def call(kernel, shape, *operands, name, flops=0):
        return pl.pallas_call(
            kernel,
            out_shape=jax.ShapeDtypeStruct(*shape),
            in_specs=[VMEM] * len(operands),
            out_specs=VMEM,
            compiler_params=params,
            cost_estimate=pl.CostEstimate(
                flops=flops, bytes_accessed=rows * width, transcendentals=0
            ),
            name=name,
        )(*operands)

    stack = call(stack_kernel, ((rows, width), jnp.bfloat16), *blocks, name="token_stack")
    far = [crossing(grads[distance % nlo], "dp", distance) for distance in range(2, ndp)]
    owned = count // nsub
    per = grads[0].shape[0]

    far = call(
        gather_kernel,
        ((per * (ndp - 2), width), jnp.bfloat16),
        *far,
        name="far_gradients",
        flops=FAR_COST * stack.size,
    )
    other = swap(stack, "pair", 1)
    near = call(copy_kernel, ((per, width), jnp.bfloat16), grads[-1], stack, name="near_gradient")
    near = call(
        gather_kernel,
        ((2 * per, width), jnp.bfloat16),
        grads[0],
        swap(near, "dp", 1),
        name="near_gradients",
    )

    def partial(some, name):
        return call(
            functools.partial(score_kernel, total, nsub, rank, owned, 2),
            ((nsub, some.shape[0] // (2 * rank), owned), jnp.float32),
            stack,
            other,
            some,
            name=name,
        )

    far_scores = partial(far, "far_scores")
    near_scores = partial(near, "near_scores")
    near_count = 2 * sequences
    distance = ndp // 2
    kept = (distance - 2) * sequences
    received = crossing(far_scores[:, kept:], "dp", distance)
    near_scores += received[:, :near_count]
    if kept:
        far_scores = swap(far_scores[:, :kept], "pair", 1) + received[:, near_count:]
    distance //= 2
    while distance > 1:
        kept = (distance - 2) * sequences
        received = swap(far_scores[:, kept:], "dp", distance)
        near_scores += received[:, :near_count]
        far_scores = far_scores[:, :kept] + received[:, near_count:]
        distance //= 2
    distance = nsub // 2
    while distance > 1:
        near_scores = near_scores[:distance] + swap(near_scores[distance:], "sub", distance)
        distance //= 2
    near_scores = swap(near_scores[:1], "pair", 1) + crossing(near_scores[1:], "sub", 1)
    scores = near_scores[0]
    other = crossing(scores[sequences:], "dp", 1)
    return (swap(scores[:sequences], "pair", 1) + other).T


def solution(mesh):
    placed = (
        P(("groups", "dp", "sub", "pair"), None),
        P(("groups", "dp", "sub", "pair"), None),
        P(("groups", "dp", "sub", "pair")),
        P(("groups", "dp", "pair"), None, None),
        P(("groups", "dp", "pair"), None, None),
        P(("groups", "dp", "pair")),
        P(),
        P(),
    )
    return jax.shard_map(
        per_device,
        mesh=mesh,
        in_specs=placed,
        out_specs=P(("groups", "sub"), ("dp", "pair")),
        check_vma=False,
    )
```

```python
import functools

import jax
import jax.numpy as jnp
from jax import lax
from jax.experimental import pallas as pl
from jax.experimental.pallas import tpu as pltpu
from jax.sharding import PartitionSpec as P

QMEAN = 64
EXTRA = 128
KEPT = 48
FAR_COST = 40000
VMEM = pl.BlockSpec(memory_space=pltpu.VMEM)
SMEM = pl.BlockSpec(memory_space=pltpu.SMEM)
HBM = pl.BlockSpec(memory_space=pltpu.HBM)
LIMIT = 48 * 1024 * 1024


def rows_by_rows(left, right, **kwargs):
    return lax.dot_general(
        left, right, (((1,), (1,)), ((), ())), preferred_element_type=jnp.float32, **kwargs
    )


def in_hbm(*arrays):
    return [pltpu.with_memory_space_constraint(array, pltpu.HBM) for array in arrays]


def swap(value, axis, distance):
    count = lax.axis_size(axis)
    return lax.ppermute(value, axis, [(source, source ^ distance) for source in range(count)])


def share_start(nlo, nsub, dlo, dsub, width):
    low = (lax.axis_index("dp") % nlo) ^ dlo
    part = low * nsub + (lax.axis_index("sub") ^ dsub)
    return pl.multiple_of(part * width, width)


def query_kernel(nlo, nsub, inputs, gradient, ids, down, up, *rest):
    shares, (held_inputs, held_gradient, held_ids, held_down, held_up, sems) = rest[:-6], rest[-6:]
    tokens, features = inputs.shape
    width = features // (nlo * nsub)
    copies = [
        pltpu.make_async_copy(source, target, sems.at[place])
        for place, (source, target) in enumerate(
            (
                (inputs, held_inputs),
                (down, held_down),
                (gradient, held_gradient),
                (up, held_up),
                (ids, held_ids),
            )
        )
    ]
    for copy in copies:
        copy.start()
    starts = [
        share_start(nlo, nsub, place // nsub, place % nsub, width) for place in range(len(shares))
    ]
    copies[0].wait()
    for start, share in zip(starts, shares):
        share[:, 0:width] = held_inputs[:, pl.ds(start, width)]
    for copy in copies[1:]:
        copy.wait()
    low_down, low_up = 0.0, 0.0
    for half in range(2):
        columns = pl.ds(half * features // 2, features // 2)
        low_down += rows_by_rows(held_down[:, columns], held_inputs[:, columns])
        low_up += rows_by_rows(held_up[:, columns], held_gradient[:, columns])
    for start, share in zip(starts, shares):
        share[:, width : 2 * width] = held_gradient[:, pl.ds(start, width)]
    rank = low_down.shape[0]
    id_rows = jnp.broadcast_to(held_ids[...].astype(jnp.float32), (EXTRA - 2 * rank, tokens))
    extras = jnp.concatenate([low_down, low_up, id_rows], axis=0).T.astype(jnp.bfloat16)
    for share in shares:
        share[:, 2 * width :] = extras


def training_kernel(nlo, nsub, length_source, inputs, gradient, down, up, *rest):
    outs, scratch = rest[:nlo], rest[nlo:]
    held_inputs, held_gradient, held_down, held_up, lengths, sems, map_sems = scratch
    sequences, slots, features = inputs.shape
    rows = sequences * slots
    rank = down.shape[0]
    width = features // (nlo * nsub)
    pieces = sems.shape[1]
    step = features // pieces
    maps = [
        pltpu.make_async_copy(down, held_down, map_sems.at[0]),
        pltpu.make_async_copy(up, held_up, map_sems.at[1]),
        pltpu.make_async_copy(length_source, lengths, map_sems.at[2]),
    ]
    maps[2].start()
    maps[0].start()
    maps[1].start()
    held = (held_inputs, held_gradient)
    copies = []
    for piece in range(pieces):
        columns = pl.ds(piece * step, step)
        for array, source in enumerate((inputs, gradient)):
            copy = pltpu.make_async_copy(
                source.at[:, :, columns], held[array].at[:, :, columns], sems.at[array, piece]
            )
            copy.start()
            copies.append(copy)

    maps[2].wait()
    live = jnp.concatenate(
        [
            jnp.concatenate(
                [
                    (lax.broadcasted_iota(jnp.int32, (rank, slots), 1) < lengths[row])
                    if row == column
                    else jnp.zeros((rank, slots), jnp.bool_)
                    for column in range(sequences)
                ],
                axis=1,
            ).astype(jnp.float32)
            for row in range(sequences)
        ],
        axis=0,
    )
    maps[0].wait()
    maps[1].wait()
    totals = [[0.0] * sequences, [0.0] * sequences]
    for piece in range(pieces):
        columns = pl.ds(piece * step, step)
        for copy in copies[2 * piece : 2 * piece + 2]:
            copy.wait()
        for array, weights in enumerate((held_down, held_up)):
            for row in range(sequences):
                totals[array][row] += rows_by_rows(weights[:, columns], held[array][row, :, columns])
    low = []
    for parts in totals:
        rounded = jnp.concatenate(parts, axis=1).astype(jnp.bfloat16).astype(jnp.float32)
        low.append((jnp.concatenate([rounded] * sequences, axis=0) * live).astype(jnp.bfloat16))

    for place, out in enumerate(outs):
        columns = pl.ds(share_start(nlo, nsub, place, 0, width), width)
        for half, (factor, target) in enumerate(((low[0], held_gradient), (low[1], held_inputs))):
            product = jnp.dot(
                factor,
                target[:, :, columns].reshape(rows, width),
                preferred_element_type=jnp.float32,
            )
            out[half * sequences * rank : (half + 1) * sequences * rank, :] = product.astype(
                jnp.bfloat16
            )


def stack_kernel(*refs):
    blocks, out = refs[:-1], refs[-1]
    tokens = blocks[0].shape[0]
    width = out.shape[1]
    total = len(blocks) * tokens
    extras = []
    for place, block in enumerate(blocks):
        out[place * tokens : (place + 1) * tokens, :] = block[:, 0:width]
        start = total + place * tokens
        out[start : start + tokens, :] = block[:, width : 2 * width]
        extras.append(block[:, 2 * width :].astype(jnp.float32).T[:KEPT].astype(jnp.bfloat16))
    chunk = min(width, total)
    for place in range(total // chunk):
        some = extras[place * chunk // tokens : (place + 1) * chunk // tokens]
        start = 2 * total + place * KEPT
        out[start : start + KEPT, 0:chunk] = jnp.concatenate(some, axis=1)


def gather_kernel(*refs):
    blocks, out = refs[:-1], refs[-1]
    for place, block in enumerate(blocks):
        half = block.shape[0] // 2
        out[place * half : (place + 1) * half, :] = block[:half, :]
        start = (len(blocks) + place) * half
        out[start : start + half, :] = block[half:, :]


def copy_kernel(source, _, target):
    target[...] = source[...]


def score_kernel(total, nsub, rank, owned, stacks, *refs):
    token_refs, grads, out = refs[:stacks], refs[stacks], refs[-1]
    chunk = min(total, token_refs[0].shape[1])
    per = grads.shape[0] // 2
    sequences = per // rank
    grad_down, grad_up = grads[:per], grads[per:]
    number = lax.broadcasted_iota(jnp.int32, (owned, total), 0)
    scores = [jnp.zeros((sequences, owned), jnp.float32)] * nsub
    for stack in token_refs:
        extras = jnp.concatenate(
            [
                stack[2 * total + place * KEPT : 2 * total + (place + 1) * KEPT, 0:chunk]
                for place in range(total // chunk)
            ],
            axis=1,
        ).astype(jnp.float32)
        low_down, low_up = extras[:rank], extras[rank : 2 * rank]
        ids = extras[2 * rank : 2 * rank + 1].astype(jnp.int32)
        product = rows_by_rows(grad_down, stack[total : 2 * total, :]).reshape(
            sequences, rank, total
        ) * low_down[None]
        product += rows_by_rows(grad_up, stack[0:total, :]).reshape(
            sequences, rank, total
        ) * low_up[None]
        per_token = jnp.sum(product, axis=1)
        for place in range(nsub):
            first = (place ^ lax.axis_index("sub")) * owned
            one_hot = (ids == number + first).astype(jnp.float32)
            scores[place] += rows_by_rows(per_token, one_hot, precision=lax.Precision.HIGHEST)
    for place in range(nsub):
        out[place] = scores[place]


def per_device(
    query_inputs,
    query_gradient,
    query_sequence_index,
    training_inputs,
    training_gradient,
    training_length,
    adapter_down_map,
    adapter_up_map,
):
    tokens, features = query_inputs.shape
    sequences, slots, _ = training_inputs.shape
    rank = adapter_down_map.shape[1]
    ndp, nsub, npair = (lax.axis_size(name) for name in ("dp", "sub", "pair"))
    nlo = 2
    width = features // (nlo * nsub)
    count = tokens * ndp * nsub * npair // QMEAN
    down, up = adapter_down_map.T, adapter_up_map.T
    params = pltpu.CompilerParams(vmem_limit_bytes=LIMIT)

    def crossing(value, axis, distance):
        pairs = [
            (i * npair + k, (i ^ distance) * npair + (k ^ 1))
            for i in range(lax.axis_size(axis))
            for k in range(npair)
        ]
        return lax.ppermute(value, (axis, "pair"), pairs)

    shares = pl.pallas_call(
        functools.partial(query_kernel, nlo, nsub),
        out_shape=[jax.ShapeDtypeStruct((tokens, 2 * width + EXTRA), jnp.bfloat16)] * (nlo * nsub),
        in_specs=[HBM] * 5,
        out_specs=[VMEM] * (nlo * nsub),
        scratch_shapes=[
            pltpu.VMEM((tokens, features), jnp.bfloat16),
            pltpu.VMEM((tokens, features), jnp.bfloat16),
            pltpu.VMEM((1, tokens), jnp.int32),
            pltpu.VMEM((rank, features), jnp.bfloat16),
            pltpu.VMEM((rank, features), jnp.bfloat16),
            pltpu.SemaphoreType.DMA((5,)),
        ],
        compiler_params=params,
        name="query_shares",
    )(*in_hbm(query_inputs, query_gradient, query_sequence_index.reshape(1, tokens), down, up))
    blocks = [shares[0]]
    for place in sorted(range(1, nlo * nsub), key=lambda place: (place != nsub, place > nsub)):
        dlo, dsub = place // nsub, place % nsub
        flip = dlo & (dsub > 0)
        pairs = []
        for i in range(ndp):
            for j in range(nsub):
                for k in range(npair):
                    target = ((i ^ dlo) * nsub + (j ^ dsub)) * npair + (k ^ flip)
                    pairs.append(((i * nsub + j) * npair + k, target))
        blocks.append(lax.ppermute(shares[place], ("dp", "sub", "pair"), pairs))

    grads = pl.pallas_call(
        functools.partial(training_kernel, nlo, nsub),
        out_shape=[jax.ShapeDtypeStruct((2 * sequences * rank, width), jnp.bfloat16)] * nlo,
        in_specs=[HBM] * 5,
        out_specs=[VMEM] * nlo,
        scratch_shapes=[
            pltpu.VMEM((sequences, slots, features), jnp.bfloat16),
            pltpu.VMEM((sequences, slots, features), jnp.bfloat16),
            pltpu.VMEM((rank, features), jnp.bfloat16),
            pltpu.VMEM((rank, features), jnp.bfloat16),
            pltpu.SMEM((sequences,), jnp.int32),
            pltpu.SemaphoreType.DMA((2, 2)),
            pltpu.SemaphoreType.DMA((3,)),
        ],
        cost_estimate=pl.CostEstimate(
            flops=12 * sequences * slots * features * rank,
            bytes_accessed=12 * sequences * slots * features,
            transcendentals=0,
        ),
        compiler_params=params,
        name="training_gradients",
    )(*in_hbm(training_length, training_inputs, training_gradient, down, up))
    nblocks = nlo * nsub
    total = nblocks * tokens
    rows = 2 * total + KEPT * max(1, total // width)
    def call(kernel, shape, *operands, name, flops=0):
        return pl.pallas_call(
            kernel,
            out_shape=jax.ShapeDtypeStruct(*shape),
            in_specs=[VMEM] * len(operands),
            out_specs=VMEM,
            compiler_params=params,
            cost_estimate=pl.CostEstimate(
                flops=flops, bytes_accessed=rows * width, transcendentals=0
            ),
            name=name,
        )(*operands)

    stack = call(stack_kernel, ((rows, width), jnp.bfloat16), *blocks, name="token_stack")
    far = [crossing(grads[distance % nlo], "dp", distance) for distance in range(2, ndp)]
    owned = count // nsub
    per = grads[0].shape[0]

    far = call(
        gather_kernel,
        ((per * (ndp - 2), width), jnp.bfloat16),
        *far,
        name="far_gradients",
        flops=FAR_COST * stack.size,
    )
    other = swap(stack, "pair", 1)
    near = call(copy_kernel, ((per, width), jnp.bfloat16), grads[-1], stack, name="near_gradient")
    near = call(
        gather_kernel,
        ((2 * per, width), jnp.bfloat16),
        grads[0],
        swap(near, "dp", 1),
        name="near_gradients",
    )

    def partial(some, name):
        return call(
            functools.partial(score_kernel, total, nsub, rank, owned, 2),
            ((nsub, some.shape[0] // (2 * rank), owned), jnp.float32),
            stack,
            other,
            some,
            name=name,
        )

    far_scores = partial(far, "far_scores")
    near_scores = partial(near, "near_scores")
    near_count = 2 * sequences
    distance = ndp // 2
    kept = (distance - 2) * sequences
    received = crossing(far_scores[:, kept:], "dp", distance)
    near_scores += received[:, :near_count]
    if kept:
        far_scores = swap(far_scores[:, :kept], "pair", 1) + received[:, near_count:]
    distance //= 2
    while distance > 1:
        kept = (distance - 2) * sequences
        received = swap(far_scores[:, kept:], "dp", distance)
        near_scores += received[:, :near_count]
        far_scores = far_scores[:, :kept] + received[:, near_count:]
        distance //= 2
    distance = nsub // 2
    while distance > 1:
        near_scores = near_scores[:distance] + swap(near_scores[distance:], "sub", distance)
        distance //= 2
    near_scores = swap(near_scores[:1], "pair", 1) + crossing(near_scores[1:], "sub", 1)
    scores = near_scores[0]
    other = crossing(scores[sequences:], "dp", 1)
    return (swap(scores[:sequences], "pair", 1) + other).T


def solution(mesh):
    placed = (
        P(("groups", "dp", "sub", "pair"), None),
        P(("groups", "dp", "sub", "pair"), None),
        P(("groups", "dp", "sub", "pair")),
        P(("groups", "dp", "pair"), None, None),
        P(("groups", "dp", "pair"), None, None),
        P(("groups", "dp", "pair")),
        P(),
        P(),
    )
    return jax.shard_map(
        per_device,
        mesh=mesh,
        in_specs=placed,
        out_specs=P(("groups", "sub"), ("dp", "pair")),
        check_vma=False,
    )
```

```python
import functools

import jax
import jax.numpy as jnp
from jax import lax
from jax.experimental import pallas as pl
from jax.experimental.pallas import tpu as pltpu
from jax.sharding import PartitionSpec as P

QMEAN = 64
EXTRA = 128
KEPT = 48
FAR_COST = 40000
VMEM = pl.BlockSpec(memory_space=pltpu.VMEM)
SMEM = pl.BlockSpec(memory_space=pltpu.SMEM)
HBM = pl.BlockSpec(memory_space=pltpu.HBM)
LIMIT = 48 * 1024 * 1024


def rows_by_rows(left, right, **kwargs):
    return lax.dot_general(
        left, right, (((1,), (1,)), ((), ())), preferred_element_type=jnp.float32, **kwargs
    )


def in_hbm(*arrays):
    return [pltpu.with_memory_space_constraint(array, pltpu.HBM) for array in arrays]


def swap(value, axis, distance):
    count = lax.axis_size(axis)
    return lax.ppermute(value, axis, [(source, source ^ distance) for source in range(count)])


def share_start(nlo, nsub, dlo, dsub, width):
    low = (lax.axis_index("dp") % nlo) ^ dlo
    part = low * nsub + (lax.axis_index("sub") ^ dsub)
    return pl.multiple_of(part * width, width)


def query_kernel(nlo, nsub, inputs, gradient, ids, down, up, *rest):
    shares, (held_inputs, held_gradient, held_ids, held_down, held_up, sems) = rest[:-6], rest[-6:]
    tokens, features = inputs.shape
    width = features // (nlo * nsub)
    copies = [
        pltpu.make_async_copy(source, target, sems.at[place])
        for place, (source, target) in enumerate(
            (
                (inputs, held_inputs),
                (down, held_down),
                (gradient, held_gradient),
                (up, held_up),
                (ids, held_ids),
            )
        )
    ]
    for copy in copies:
        copy.start()
    starts = [
        share_start(nlo, nsub, place // nsub, place % nsub, width) for place in range(len(shares))
    ]
    copies[0].wait()
    for start, share in zip(starts, shares):
        share[:, 0:width] = held_inputs[:, pl.ds(start, width)]
    for copy in copies[1:]:
        copy.wait()
    low_down, low_up = 0.0, 0.0
    for half in range(2):
        columns = pl.ds(half * features // 2, features // 2)
        low_down += rows_by_rows(held_down[:, columns], held_inputs[:, columns])
        low_up += rows_by_rows(held_up[:, columns], held_gradient[:, columns])
    for start, share in zip(starts, shares):
        share[:, width : 2 * width] = held_gradient[:, pl.ds(start, width)]
    rank = low_down.shape[0]
    id_rows = jnp.broadcast_to(held_ids[...].astype(jnp.float32), (KEPT - 2 * rank, tokens))
    extras = jnp.concatenate([low_down, low_up, id_rows], axis=0).astype(jnp.bfloat16)
    for share in shares:
        share[:, 2 * width :] = jnp.zeros((tokens, EXTRA), jnp.bfloat16)
        share[0:KEPT, 2 * width : 2 * width + tokens] = extras


def training_kernel(nlo, nsub, length_source, inputs, gradient, down, up, *rest):
    outs, scratch = rest[:nlo], rest[nlo:]
    held_inputs, held_gradient, held_down, held_up, lengths, sems, map_sems = scratch
    sequences, slots, features = inputs.shape
    rows = sequences * slots
    rank = down.shape[0]
    width = features // (nlo * nsub)
    pieces = sems.shape[1]
    step = features // pieces
    maps = [
        pltpu.make_async_copy(down, held_down, map_sems.at[0]),
        pltpu.make_async_copy(up, held_up, map_sems.at[1]),
        pltpu.make_async_copy(length_source, lengths, map_sems.at[2]),
    ]
    maps[2].start()
    maps[0].start()
    maps[1].start()
    held = (held_inputs, held_gradient)
    copies = []
    for piece in range(pieces):
        columns = pl.ds(piece * step, step)
        for array, source in enumerate((inputs, gradient)):
            copy = pltpu.make_async_copy(
                source.at[:, :, columns], held[array].at[:, :, columns], sems.at[array, piece]
            )
            copy.start()
            copies.append(copy)

    maps[2].wait()
    live = jnp.concatenate(
        [
            jnp.concatenate(
                [
                    (lax.broadcasted_iota(jnp.int32, (rank, slots), 1) < lengths[row])
                    if row == column
                    else jnp.zeros((rank, slots), jnp.bool_)
                    for column in range(sequences)
                ],
                axis=1,
            ).astype(jnp.float32)
            for row in range(sequences)
        ],
        axis=0,
    )
    maps[0].wait()
    maps[1].wait()
    totals = [[0.0] * sequences, [0.0] * sequences]
    for piece in range(pieces):
        columns = pl.ds(piece * step, step)
        for copy in copies[2 * piece : 2 * piece + 2]:
            copy.wait()
        for array, weights in enumerate((held_down, held_up)):
            for row in range(sequences):
                totals[array][row] += rows_by_rows(weights[:, columns], held[array][row, :, columns])
    low = []
    for parts in totals:
        rounded = jnp.concatenate(parts, axis=1).astype(jnp.bfloat16).astype(jnp.float32)
        low.append((jnp.concatenate([rounded] * sequences, axis=0) * live).astype(jnp.bfloat16))

    for place, out in enumerate(outs):
        columns = pl.ds(share_start(nlo, nsub, place, 0, width), width)
        for half, (factor, target) in enumerate(((low[0], held_gradient), (low[1], held_inputs))):
            product = jnp.dot(
                factor,
                target[:, :, columns].reshape(rows, width),
                preferred_element_type=jnp.float32,
            )
            out[half * sequences * rank : (half + 1) * sequences * rank, :] = product.astype(
                jnp.bfloat16
            )


def stack_kernel(*refs):
    blocks, out = refs[:-1], refs[-1]
    tokens = blocks[0].shape[0]
    width = out.shape[1]
    total = len(blocks) * tokens
    extras = []
    for place, block in enumerate(blocks):
        out[place * tokens : (place + 1) * tokens, :] = block[:, 0:width]
        start = total + place * tokens
        out[start : start + tokens, :] = block[:, width : 2 * width]
        extras.append(block[0:KEPT, 2 * width : 2 * width + tokens])
    chunk = min(width, total)
    for place in range(total // chunk):
        some = extras[place * chunk // tokens : (place + 1) * chunk // tokens]
        start = 2 * total + place * KEPT
        out[start : start + KEPT, 0:chunk] = jnp.concatenate(some, axis=1)


def gather_kernel(*refs):
    blocks, out = refs[:-1], refs[-1]
    for place, block in enumerate(blocks):
        half = block.shape[0] // 2
        out[place * half : (place + 1) * half, :] = block[:half, :]
        start = (len(blocks) + place) * half
        out[start : start + half, :] = block[half:, :]


def copy_kernel(source, _, target):
    target[...] = source[...]


def score_kernel(total, nsub, rank, owned, stacks, *refs):
    token_refs, grads, out = refs[:stacks], refs[stacks], refs[-1]
    chunk = min(total, token_refs[0].shape[1])
    per = grads.shape[0] // 2
    sequences = per // rank
    grad_down, grad_up = grads[:per], grads[per:]
    number = lax.broadcasted_iota(jnp.int32, (owned, total), 0)
    scores = [jnp.zeros((sequences, owned), jnp.float32)] * nsub
    for stack in token_refs:
        extras = jnp.concatenate(
            [
                stack[2 * total + place * KEPT : 2 * total + (place + 1) * KEPT, 0:chunk]
                for place in range(total // chunk)
            ],
            axis=1,
        ).astype(jnp.float32)
        low_down, low_up = extras[:rank], extras[rank : 2 * rank]
        ids = extras[2 * rank : 2 * rank + 1].astype(jnp.int32)
        product = rows_by_rows(grad_down, stack[total : 2 * total, :]).reshape(
            sequences, rank, total
        ) * low_down[None]
        product += rows_by_rows(grad_up, stack[0:total, :]).reshape(
            sequences, rank, total
        ) * low_up[None]
        per_token = jnp.sum(product, axis=1)
        for place in range(nsub):
            first = (place ^ lax.axis_index("sub")) * owned
            one_hot = (ids == number + first).astype(jnp.float32)
            scores[place] += rows_by_rows(per_token, one_hot, precision=lax.Precision.HIGHEST)
    for place in range(nsub):
        out[place] = scores[place]


def per_device(
    query_inputs,
    query_gradient,
    query_sequence_index,
    training_inputs,
    training_gradient,
    training_length,
    adapter_down_map,
    adapter_up_map,
):
    tokens, features = query_inputs.shape
    sequences, slots, _ = training_inputs.shape
    rank = adapter_down_map.shape[1]
    ndp, nsub, npair = (lax.axis_size(name) for name in ("dp", "sub", "pair"))
    nlo = 2
    width = features // (nlo * nsub)
    count = tokens * ndp * nsub * npair // QMEAN
    down, up = adapter_down_map.T, adapter_up_map.T
    params = pltpu.CompilerParams(vmem_limit_bytes=LIMIT)

    def crossing(value, axis, distance):
        pairs = [
            (i * npair + k, (i ^ distance) * npair + (k ^ 1))
            for i in range(lax.axis_size(axis))
            for k in range(npair)
        ]
        return lax.ppermute(value, (axis, "pair"), pairs)

    shares = pl.pallas_call(
        functools.partial(query_kernel, nlo, nsub),
        out_shape=[jax.ShapeDtypeStruct((tokens, 2 * width + EXTRA), jnp.bfloat16)] * (nlo * nsub),
        in_specs=[HBM] * 5,
        out_specs=[VMEM] * (nlo * nsub),
        scratch_shapes=[
            pltpu.VMEM((tokens, features), jnp.bfloat16),
            pltpu.VMEM((tokens, features), jnp.bfloat16),
            pltpu.VMEM((1, tokens), jnp.int32),
            pltpu.VMEM((rank, features), jnp.bfloat16),
            pltpu.VMEM((rank, features), jnp.bfloat16),
            pltpu.SemaphoreType.DMA((5,)),
        ],
        compiler_params=params,
        name="query_shares",
    )(*in_hbm(query_inputs, query_gradient, query_sequence_index.reshape(1, tokens), down, up))
    blocks = [shares[0]]
    for place in sorted(range(1, nlo * nsub), key=lambda place: (place != nsub, place > nsub)):
        dlo, dsub = place // nsub, place % nsub
        flip = dlo & (dsub > 0)
        pairs = []
        for i in range(ndp):
            for j in range(nsub):
                for k in range(npair):
                    target = ((i ^ dlo) * nsub + (j ^ dsub)) * npair + (k ^ flip)
                    pairs.append(((i * nsub + j) * npair + k, target))
        blocks.append(lax.ppermute(shares[place], ("dp", "sub", "pair"), pairs))

    grads = pl.pallas_call(
        functools.partial(training_kernel, nlo, nsub),
        out_shape=[jax.ShapeDtypeStruct((2 * sequences * rank, width), jnp.bfloat16)] * nlo,
        in_specs=[HBM] * 5,
        out_specs=[VMEM] * nlo,
        scratch_shapes=[
            pltpu.VMEM((sequences, slots, features), jnp.bfloat16),
            pltpu.VMEM((sequences, slots, features), jnp.bfloat16),
            pltpu.VMEM((rank, features), jnp.bfloat16),
            pltpu.VMEM((rank, features), jnp.bfloat16),
            pltpu.SMEM((sequences,), jnp.int32),
            pltpu.SemaphoreType.DMA((2, 2)),
            pltpu.SemaphoreType.DMA((3,)),
        ],
        cost_estimate=pl.CostEstimate(
            flops=12 * sequences * slots * features * rank,
            bytes_accessed=12 * sequences * slots * features,
            transcendentals=0,
        ),
        compiler_params=params,
        name="training_gradients",
    )(*in_hbm(training_length, training_inputs, training_gradient, down, up))
    nblocks = nlo * nsub
    total = nblocks * tokens
    rows = 2 * total + KEPT * max(1, total // width)
    def call(kernel, shape, *operands, name, flops=0):
        return pl.pallas_call(
            kernel,
            out_shape=jax.ShapeDtypeStruct(*shape),
            in_specs=[VMEM] * len(operands),
            out_specs=VMEM,
            compiler_params=params,
            cost_estimate=pl.CostEstimate(
                flops=flops, bytes_accessed=rows * width, transcendentals=0
            ),
            name=name,
        )(*operands)

    stack = call(stack_kernel, ((rows, width), jnp.bfloat16), *blocks, name="token_stack")
    far = [crossing(grads[distance % nlo], "dp", distance) for distance in range(2, ndp)]
    owned = count // nsub
    per = grads[0].shape[0]

    far = call(
        gather_kernel,
        ((per * (ndp - 2), width), jnp.bfloat16),
        *far,
        name="far_gradients",
        flops=FAR_COST * stack.size,
    )
    other = swap(stack, "pair", 1)
    near = call(copy_kernel, ((per, width), jnp.bfloat16), grads[-1], stack, name="near_gradient")
    near = call(
        gather_kernel,
        ((2 * per, width), jnp.bfloat16),
        grads[0],
        swap(near, "dp", 1),
        name="near_gradients",
    )

    def partial(some, name):
        return call(
            functools.partial(score_kernel, total, nsub, rank, owned, 2),
            ((nsub, some.shape[0] // (2 * rank), owned), jnp.float32),
            stack,
            other,
            some,
            name=name,
        )

    far_scores = partial(far, "far_scores")
    near_scores = partial(near, "near_scores")
    near_count = 2 * sequences
    distance = ndp // 2
    kept = (distance - 2) * sequences
    received = crossing(far_scores[:, kept:], "dp", distance)
    near_scores += received[:, :near_count]
    if kept:
        far_scores = swap(far_scores[:, :kept], "pair", 1) + received[:, near_count:]
    distance //= 2
    while distance > 1:
        kept = (distance - 2) * sequences
        received = swap(far_scores[:, kept:], "dp", distance)
        near_scores += received[:, :near_count]
        far_scores = far_scores[:, :kept] + received[:, near_count:]
        distance //= 2
    distance = nsub // 2
    while distance > 1:
        near_scores = near_scores[:distance] + swap(near_scores[distance:], "sub", distance)
        distance //= 2
    near_scores = swap(near_scores[:1], "pair", 1) + crossing(near_scores[1:], "sub", 1)
    scores = near_scores[0]
    other = crossing(scores[sequences:], "dp", 1)
    return (swap(scores[:sequences], "pair", 1) + other).T


def solution(mesh):
    placed = (
        P(("groups", "dp", "sub", "pair"), None),
        P(("groups", "dp", "sub", "pair"), None),
        P(("groups", "dp", "sub", "pair")),
        P(("groups", "dp", "pair"), None, None),
        P(("groups", "dp", "pair"), None, None),
        P(("groups", "dp", "pair")),
        P(),
        P(),
    )
    return jax.shard_map(
        per_device,
        mesh=mesh,
        in_specs=placed,
        out_specs=P(("groups", "sub"), ("dp", "pair")),
        check_vma=False,
    )
```

```python
import functools

import jax
import jax.numpy as jnp
from jax import lax
from jax.experimental import pallas as pl
from jax.experimental.pallas import tpu as pltpu
from jax.sharding import PartitionSpec as P

QMEAN = 64
EXTRA = 128
KEPT = 48
FAR_COST = 40000
VMEM = pl.BlockSpec(memory_space=pltpu.VMEM)
SMEM = pl.BlockSpec(memory_space=pltpu.SMEM)
HBM = pl.BlockSpec(memory_space=pltpu.HBM)
LIMIT = 48 * 1024 * 1024


def rows_by_rows(left, right, **kwargs):
    return lax.dot_general(
        left, right, (((1,), (1,)), ((), ())), preferred_element_type=jnp.float32, **kwargs
    )


def in_hbm(*arrays):
    return [pltpu.with_memory_space_constraint(array, pltpu.HBM) for array in arrays]


def swap(value, axis, distance):
    count = lax.axis_size(axis)
    return lax.ppermute(value, axis, [(source, source ^ distance) for source in range(count)])


def share_start(nlo, nsub, dlo, dsub, width):
    low = (lax.axis_index("dp") % nlo) ^ dlo
    part = low * nsub + (lax.axis_index("sub") ^ dsub)
    return pl.multiple_of(part * width, width)


def query_kernel(nlo, nsub, inputs, gradient, ids, down, up, *rest):
    shares, (held_inputs, held_gradient, held_ids, held_down, held_up, sems) = rest[:-6], rest[-6:]
    tokens, features = inputs.shape
    width = features // (nlo * nsub)
    copies = [
        pltpu.make_async_copy(source, target, sems.at[place])
        for place, (source, target) in enumerate(
            (
                (inputs, held_inputs),
                (down, held_down),
                (gradient, held_gradient),
                (up, held_up),
                (ids, held_ids),
            )
        )
    ]
    for copy in copies:
        copy.start()
    starts = [
        share_start(nlo, nsub, place // nsub, place % nsub, width) for place in range(len(shares))
    ]
    for share in shares:
        share[:, 2 * width :] = jnp.zeros((tokens, EXTRA), jnp.bfloat16)
    copies[0].wait()
    for start, share in zip(starts, shares):
        share[:, 0:width] = held_inputs[:, pl.ds(start, width)]
    for copy in copies[1:]:
        copy.wait()
    low_down, low_up = 0.0, 0.0
    for half in range(2):
        columns = pl.ds(half * features // 2, features // 2)
        low_down += rows_by_rows(held_down[:, columns], held_inputs[:, columns])
        low_up += rows_by_rows(held_up[:, columns], held_gradient[:, columns])
    for start, share in zip(starts, shares):
        share[:, width : 2 * width] = held_gradient[:, pl.ds(start, width)]
    rank = low_down.shape[0]
    id_rows = jnp.broadcast_to(held_ids[...].astype(jnp.float32), (KEPT - 2 * rank, tokens))
    extras = jnp.concatenate([low_down, low_up, id_rows], axis=0).astype(jnp.bfloat16)
    for share in shares:
        share[0:KEPT, 2 * width : 2 * width + tokens] = extras


def training_kernel(nlo, nsub, length_source, inputs, gradient, down, up, *rest):
    outs, scratch = rest[:nlo], rest[nlo:]
    held_inputs, held_gradient, held_down, held_up, lengths, sems, map_sems = scratch
    sequences, slots, features = inputs.shape
    rows = sequences * slots
    rank = down.shape[0]
    width = features // (nlo * nsub)
    pieces = sems.shape[1]
    step = features // pieces
    maps = [
        pltpu.make_async_copy(down, held_down, map_sems.at[0]),
        pltpu.make_async_copy(up, held_up, map_sems.at[1]),
        pltpu.make_async_copy(length_source, lengths, map_sems.at[2]),
    ]
    maps[2].start()
    maps[0].start()
    maps[1].start()
    held = (held_inputs, held_gradient)
    copies = []
    for piece in range(pieces):
        columns = pl.ds(piece * step, step)
        for array, source in enumerate((inputs, gradient)):
            copy = pltpu.make_async_copy(
                source.at[:, :, columns], held[array].at[:, :, columns], sems.at[array, piece]
            )
            copy.start()
            copies.append(copy)

    maps[2].wait()
    live = jnp.concatenate(
        [
            jnp.concatenate(
                [
                    (lax.broadcasted_iota(jnp.int32, (rank, slots), 1) < lengths[row])
                    if row == column
                    else jnp.zeros((rank, slots), jnp.bool_)
                    for column in range(sequences)
                ],
                axis=1,
            ).astype(jnp.float32)
            for row in range(sequences)
        ],
        axis=0,
    )
    maps[0].wait()
    maps[1].wait()
    totals = [[0.0] * sequences, [0.0] * sequences]
    for piece in range(pieces):
        columns = pl.ds(piece * step, step)
        for copy in copies[2 * piece : 2 * piece + 2]:
            copy.wait()
        for array, weights in enumerate((held_down, held_up)):
            for row in range(sequences):
                totals[array][row] += rows_by_rows(weights[:, columns], held[array][row, :, columns])
    low = []
    for parts in totals:
        rounded = jnp.concatenate(parts, axis=1).astype(jnp.bfloat16).astype(jnp.float32)
        low.append((jnp.concatenate([rounded] * sequences, axis=0) * live).astype(jnp.bfloat16))

    for place, out in enumerate(outs):
        columns = pl.ds(share_start(nlo, nsub, place, 0, width), width)
        for half, (factor, target) in enumerate(((low[0], held_gradient), (low[1], held_inputs))):
            product = jnp.dot(
                factor,
                target[:, :, columns].reshape(rows, width),
                preferred_element_type=jnp.float32,
            )
            out[half * sequences * rank : (half + 1) * sequences * rank, :] = product.astype(
                jnp.bfloat16
            )


def stack_kernel(*refs):
    blocks, out = refs[:-1], refs[-1]
    tokens = blocks[0].shape[0]
    width = out.shape[1]
    total = len(blocks) * tokens
    extras = []
    for place, block in enumerate(blocks):
        out[place * tokens : (place + 1) * tokens, :] = block[:, 0:width]
        start = total + place * tokens
        out[start : start + tokens, :] = block[:, width : 2 * width]
        extras.append(block[0:KEPT, 2 * width : 2 * width + tokens])
    chunk = min(width, total)
    for place in range(total // chunk):
        some = extras[place * chunk // tokens : (place + 1) * chunk // tokens]
        start = 2 * total + place * KEPT
        out[start : start + KEPT, 0:chunk] = jnp.concatenate(some, axis=1)


def gather_kernel(*refs):
    blocks, out = refs[:-1], refs[-1]
    for place, block in enumerate(blocks):
        half = block.shape[0] // 2
        out[place * half : (place + 1) * half, :] = block[:half, :]
        start = (len(blocks) + place) * half
        out[start : start + half, :] = block[half:, :]


def copy_kernel(source, _, target):
    target[...] = source[...]


def score_kernel(total, nsub, rank, owned, stacks, *refs):
    token_refs, grads, out = refs[:stacks], refs[stacks], refs[-1]
    chunk = min(total, token_refs[0].shape[1])
    per = grads.shape[0] // 2
    sequences = per // rank
    grad_down, grad_up = grads[:per], grads[per:]
    number = lax.broadcasted_iota(jnp.int32, (owned, total), 0)
    scores = [jnp.zeros((sequences, owned), jnp.float32)] * nsub
    for stack in token_refs:
        extras = jnp.concatenate(
            [
                stack[2 * total + place * KEPT : 2 * total + (place + 1) * KEPT, 0:chunk]
                for place in range(total // chunk)
            ],
            axis=1,
        ).astype(jnp.float32)
        low_down, low_up = extras[:rank], extras[rank : 2 * rank]
        ids = extras[2 * rank : 2 * rank + 1].astype(jnp.int32)
        product = rows_by_rows(grad_down, stack[total : 2 * total, :]).reshape(
            sequences, rank, total
        ) * low_down[None]
        product += rows_by_rows(grad_up, stack[0:total, :]).reshape(
            sequences, rank, total
        ) * low_up[None]
        per_token = jnp.sum(product, axis=1)
        for place in range(nsub):
            first = (place ^ lax.axis_index("sub")) * owned
            one_hot = (ids == number + first).astype(jnp.float32)
            scores[place] += rows_by_rows(per_token, one_hot, precision=lax.Precision.HIGHEST)
    for place in range(nsub):
        out[place] = scores[place]


def per_device(
    query_inputs,
    query_gradient,
    query_sequence_index,
    training_inputs,
    training_gradient,
    training_length,
    adapter_down_map,
    adapter_up_map,
):
    tokens, features = query_inputs.shape
    sequences, slots, _ = training_inputs.shape
    rank = adapter_down_map.shape[1]
    ndp, nsub, npair = (lax.axis_size(name) for name in ("dp", "sub", "pair"))
    nlo = 2
    width = features // (nlo * nsub)
    count = tokens * ndp * nsub * npair // QMEAN
    down, up = adapter_down_map.T, adapter_up_map.T
    params = pltpu.CompilerParams(vmem_limit_bytes=LIMIT)

    def crossing(value, axis, distance):
        pairs = [
            (i * npair + k, (i ^ distance) * npair + (k ^ 1))
            for i in range(lax.axis_size(axis))
            for k in range(npair)
        ]
        return lax.ppermute(value, (axis, "pair"), pairs)

    shares = pl.pallas_call(
        functools.partial(query_kernel, nlo, nsub),
        out_shape=[jax.ShapeDtypeStruct((tokens, 2 * width + EXTRA), jnp.bfloat16)] * (nlo * nsub),
        in_specs=[HBM] * 5,
        out_specs=[VMEM] * (nlo * nsub),
        scratch_shapes=[
            pltpu.VMEM((tokens, features), jnp.bfloat16),
            pltpu.VMEM((tokens, features), jnp.bfloat16),
            pltpu.VMEM((1, tokens), jnp.int32),
            pltpu.VMEM((rank, features), jnp.bfloat16),
            pltpu.VMEM((rank, features), jnp.bfloat16),
            pltpu.SemaphoreType.DMA((5,)),
        ],
        compiler_params=params,
        name="query_shares",
    )(*in_hbm(query_inputs, query_gradient, query_sequence_index.reshape(1, tokens), down, up))
    blocks = [shares[0]]
    for place in sorted(range(1, nlo * nsub), key=lambda place: (place != nsub, place > nsub)):
        dlo, dsub = place // nsub, place % nsub
        flip = dlo & (dsub > 0)
        pairs = []
        for i in range(ndp):
            for j in range(nsub):
                for k in range(npair):
                    target = ((i ^ dlo) * nsub + (j ^ dsub)) * npair + (k ^ flip)
                    pairs.append(((i * nsub + j) * npair + k, target))
        blocks.append(lax.ppermute(shares[place], ("dp", "sub", "pair"), pairs))

    grads = pl.pallas_call(
        functools.partial(training_kernel, nlo, nsub),
        out_shape=[jax.ShapeDtypeStruct((2 * sequences * rank, width), jnp.bfloat16)] * nlo,
        in_specs=[HBM] * 5,
        out_specs=[VMEM] * nlo,
        scratch_shapes=[
            pltpu.VMEM((sequences, slots, features), jnp.bfloat16),
            pltpu.VMEM((sequences, slots, features), jnp.bfloat16),
            pltpu.VMEM((rank, features), jnp.bfloat16),
            pltpu.VMEM((rank, features), jnp.bfloat16),
            pltpu.SMEM((sequences,), jnp.int32),
            pltpu.SemaphoreType.DMA((2, 2)),
            pltpu.SemaphoreType.DMA((3,)),
        ],
        cost_estimate=pl.CostEstimate(
            flops=12 * sequences * slots * features * rank,
            bytes_accessed=12 * sequences * slots * features,
            transcendentals=0,
        ),
        compiler_params=params,
        name="training_gradients",
    )(*in_hbm(training_length, training_inputs, training_gradient, down, up))
    nblocks = nlo * nsub
    total = nblocks * tokens
    rows = 2 * total + KEPT * max(1, total // width)
    def call(kernel, shape, *operands, name, flops=0):
        return pl.pallas_call(
            kernel,
            out_shape=jax.ShapeDtypeStruct(*shape),
            in_specs=[VMEM] * len(operands),
            out_specs=VMEM,
            compiler_params=params,
            cost_estimate=pl.CostEstimate(
                flops=flops, bytes_accessed=rows * width, transcendentals=0
            ),
            name=name,
        )(*operands)

    stack = call(stack_kernel, ((rows, width), jnp.bfloat16), *blocks, name="token_stack")
    far = [crossing(grads[distance % nlo], "dp", distance) for distance in range(2, ndp)]
    owned = count // nsub
    per = grads[0].shape[0]

    far = call(
        gather_kernel,
        ((per * (ndp - 2), width), jnp.bfloat16),
        *far,
        name="far_gradients",
        flops=FAR_COST * stack.size,
    )
    other = swap(stack, "pair", 1)
    near = call(copy_kernel, ((per, width), jnp.bfloat16), grads[-1], stack, name="near_gradient")
    near = call(
        gather_kernel,
        ((2 * per, width), jnp.bfloat16),
        grads[0],
        swap(near, "dp", 1),
        name="near_gradients",
    )

    def partial(some, name):
        return call(
            functools.partial(score_kernel, total, nsub, rank, owned, 2),
            ((nsub, some.shape[0] // (2 * rank), owned), jnp.float32),
            stack,
            other,
            some,
            name=name,
        )

    far_scores = partial(far, "far_scores")
    near_scores = partial(near, "near_scores")
    near_count = 2 * sequences
    distance = ndp // 2
    kept = (distance - 2) * sequences
    received = crossing(far_scores[:, kept:], "dp", distance)
    near_scores += received[:, :near_count]
    if kept:
        far_scores = swap(far_scores[:, :kept], "pair", 1) + received[:, near_count:]
    distance //= 2
    while distance > 1:
        kept = (distance - 2) * sequences
        received = swap(far_scores[:, kept:], "dp", distance)
        near_scores += received[:, :near_count]
        far_scores = far_scores[:, :kept] + received[:, near_count:]
        distance //= 2
    distance = nsub // 2
    while distance > 1:
        near_scores = near_scores[:distance] + swap(near_scores[distance:], "sub", distance)
        distance //= 2
    near_scores = swap(near_scores[:1], "pair", 1) + crossing(near_scores[1:], "sub", 1)
    scores = near_scores[0]
    other = crossing(scores[sequences:], "dp", 1)
    return (swap(scores[:sequences], "pair", 1) + other).T


def solution(mesh):
    placed = (
        P(("groups", "dp", "sub", "pair"), None),
        P(("groups", "dp", "sub", "pair"), None),
        P(("groups", "dp", "sub", "pair")),
        P(("groups", "dp", "pair"), None, None),
        P(("groups", "dp", "pair"), None, None),
        P(("groups", "dp", "pair")),
        P(),
        P(),
    )
    return jax.shard_map(
        per_device,
        mesh=mesh,
        in_specs=placed,
        out_specs=P(("groups", "sub"), ("dp", "pair")),
        check_vma=False,
    )
```
